32 devices in a mesh: dp: 8 (over z, y), tensor: 4 (over x, core).
Axes of the slice: x: 2, y: 2, z: 4, core: 2. Of those that a mesh axis runs over, the one named last changes fastest.
Arguments:
- acts: bfloat16 [4096, 4096], P('dp'), may hold values from -0.25 to 0.25
- up_cot: bfloat16 [4096, 3584], P('dp', 'tensor'), may hold values from -6 to 6
- up_weight: bfloat16 [4096, 3584], P(None, 'tensor'), may hold values from -0.09375 to 0.09375
- error_buf: bfloat16 [8, 4096, 3584], P('dp', None, 'tensor'), may hold values from -4 to 4
- q_init: float32 [64, 3584], P(None, 'tensor'), may hold values from -6 to 6
Outputs:
- input_grad: bfloat16 [4096, 4096], P(('dp', 'tensor'))
- new_error: bfloat16 [8, 4096, 3584], P('dp', None, 'tensor')
- p_factor: float32 [64, 4096], replicated
- q_factor: float32 [64, 3584], P(None, 'tensor')
The draws below stay inside these ranges and needn't reach their ends.
All inputs are finite; a program needn't handle non-finite values.
Results may differ from the reference program's by a relative error of at most 0.001.
Values sent between devices are 32-bit elements; how exact they have to be, the bound alone decides.
A program may use at most 128 MiB of HBM per device.

```python
import jax
import jax.numpy as jnp
from jax import lax

D = 4096
RANK = 64
TOK_DEV = 512
FF = 3584
REPLICAS = 8
TOKENS = 4096
N_DP = 8


def shard_levels(key, extent, split, least, largest):
    def one(dim, blocks):
        heights = jax.random.uniform(jax.random.fold_in(jax.random.fold_in(key, 6), dim), (blocks,), jnp.float32, least / len(split), largest / len(split))
        return jnp.repeat(jnp.exp(heights), extent[dim] // blocks).reshape((-1,) + (1,) * (len(extent) - dim - 1))

    level = one(*split[0])
    for cut in split[1:]:
        level = level * one(*cut)
    return level


def gaussian(own_key, extent, spread, bound, cuts=(), kind=jnp.bfloat16):
    factor_of = shard_levels(own_key, extent, cuts, -0.22, 0.18) if cuts else 1.0
    entries = jax.random.normal(own_key, extent, jnp.float32) * spread * factor_of
    return jnp.minimum(jnp.maximum(entries, -bound), bound).astype(kind)


def setup_inputs(seed: int = 0) -> dict:
    keys = jax.random.split(jax.random.key(seed), 6)
    acts = gaussian(keys[0], (TOKENS, D), TOK_DEV ** -0.5, 0.25, ((0, 8),))
    up_cot = gaussian(keys[1], (TOKENS, FF), 1.0, 6.0, ((0, 8), (1, 4)))
    up_weight = gaussian(keys[2], (D, FF), FF ** -0.5, 0.09375, ((1, 4),))
    error_buf = gaussian(keys[3], (REPLICAS, D, FF), 0.5, 4.0, ((0, 8), (2, 4)))
    q_init = gaussian(keys[4], (RANK, FF), 1.0, 6.0, ((1, 4),), jnp.float32)
    return {"acts": acts, "up_cot": up_cot, "up_weight": up_weight, "error_buf": error_buf, "q_init": q_init}


def reference(acts, up_cot, up_weight, error_buf, q_init):
    hp = lax.Precision.HIGHEST
    input_grad = lax.dot_general(up_cot.astype(jnp.float32), up_weight.astype(jnp.float32), (((1,), (1,)), ((), ())), preferred_element_type=jnp.float32).astype(jnp.bfloat16)
    acts_r = acts.reshape(N_DP, TOK_DEV, D)
    cot_r = up_cot.reshape(N_DP, TOK_DEV, FF)

    def merge_one(items):
        xpart, cpart, epart = items
        grad = lax.dot_general(xpart.astype(jnp.float32), cpart.astype(jnp.float32), (((0,), (0,)), ((), ())), preferred_element_type=jnp.float32)
        return grad + epart.astype(jnp.float32)
    merged = lax.map(merge_one, (acts_r, cot_r, error_buf))
    left = jnp.einsum('kf,rdf->kd', q_init, merged, precision=hp)
    gram = jnp.dot(left, left.T, precision=hp)
    chol = jnp.linalg.cholesky(gram)
    basis = lax.linalg.triangular_solve(chol, left, left_side=True, lower=True)
    q_factor = jnp.einsum('kd,rdf->kf', basis, merged, precision=hp) / N_DP
    approx = jnp.einsum('kd,kf->df', basis, q_factor, precision=hp)
    new_error = (merged - approx[None]).astype(jnp.bfloat16)
    return (input_grad, new_error, basis, q_factor)
```

```python
import functools

import jax
import jax.numpy as jnp
from jax import lax
from jax.experimental import pallas as pl
from jax.experimental.pallas import tpu as pltpu
from jax.sharding import PartitionSpec as P

F32 = jnp.float32
BF16 = jnp.bfloat16
HI = lax.Precision.HIGHEST
VMEM = pltpu.VMEM
PARAMS = pltpu.CompilerParams(vmem_limit_bytes=56 * 1024 * 1024)
NT = (((1,), (1,)), ((), ()))
NN = (((1,), (0,)), ((), ()))
TN = (((0,), (0,)), ((), ()))


def dot(a, b, dims, precision=None):
    return lax.dot_general(a, b, dims, precision=precision, preferred_element_type=F32)


def halves(x):
    high = x.astype(BF16)
    low = (x - high.astype(F32)).astype(BF16)
    return high, low


def dot_split(x, b, dims):
    rows = x.shape[0]
    both = dot(jnp.concatenate(halves(x), axis=0), b, dims)
    return both[:rows] + both[rows:]


def inverse_factor(gram):
    n = gram.shape[0]
    row = lax.broadcasted_iota(jnp.int32, (n, n), 0)
    col = lax.broadcasted_iota(jnp.int32, (n, n), 1)
    work = jnp.concatenate([gram, (row == col).astype(F32)], axis=1)
    ids = lax.broadcasted_iota(jnp.int32, (n, 1), 0)
    scale = jnp.zeros((n, 1), F32)
    for k in range(n):
        pivot = work[k : k + 1, :]
        column = work[:, k : k + 1]
        d = work[k : k + 1, k : k + 1]
        scale = jnp.where(ids == k, d, scale)
        factor = jnp.where(ids > k, column / d, 0.0)
        work = work - factor * pivot
    return work[:, n:] * lax.rsqrt(scale)


def exchange_kernel(
    cfg,
    q_hbm, cot_hbm, acts_hbm, err_hbm, weight_hbm,
    grad_out, basis_out, q_out,
    q_ref, cot_ref, acts_ref, err_ref, weight_ref,
    term, core_in, x_in, dp_in, left_all,
    right_part, right_in, right_all,
    partial, partial_in, partial_x,
    load_sem, core_sem, x_sem, dp_sem, gather_sem, gx_sem, gcore_sem, r_sem, rg_sem, pc_sem, px_sem,
):
    n_dp, n_t, groups, width, qwidth, blocks, early = cfg
    n_x = n_t // 2
    rank, ff = q_ref.shape
    tokens = cot_ref.shape[0]
    rows_dp = rank // (n_dp // groups)
    me_dp, me_t = lax.axis_index("dp"), lax.axis_index("tensor")
    core, me_x = lax.rem(me_t, 2), lax.div(me_t, 2)
    mate = 1 - core
    per = rank // 8

    def send(src, dst, sems, index, dp, t):
        return pltpu.make_async_remote_copy(
            src_ref=src,
            dst_ref=dst,
            send_sem=sems.at[(0,) + index],
            recv_sem=sems.at[(1,) + index],
            device_id=(dp, t),
            device_id_type=pl.DeviceIdType.MESH,
        )

    def at_x(k):
        return lax.rem(me_x + k, n_x) * 2 + core

    def at_dp(k):
        return lax.rem(me_dp + k, n_dp)

    loads = [
        pltpu.make_async_copy(src, dst, load_sem.at[i])
        for i, (src, dst) in enumerate(
            ((q_hbm, q_ref), (cot_hbm, cot_ref), (acts_hbm, acts_ref), (err_hbm, err_ref), (weight_hbm, weight_ref))
        )
    ]
    for load in loads:
        load.start()

    barrier = pltpu.get_barrier_semaphore()
    peers = [(me_dp, me_x * 2 + mate)]
    peers += [(me_dp, at_x(k)) for k in range(1, n_x)]
    peers += [(at_dp(k), me_t) for k in range(1, n_dp)]
    for peer in peers:
        pl.semaphore_signal(barrier, inc=1, device_id=peer, device_id_type=pl.DeviceIdType.MESH)

    loads[0].wait()
    loads[1].wait()
    q_both = jnp.concatenate(halves(q_ref[...]), axis=0)
    t = dot(q_both, cot_ref[...], NT)
    t_both = jnp.concatenate(halves(t[:rank] + t[rank:]), axis=0)
    loads[2].wait()
    loads[3].wait()

    def term_block(b, half):
        x, g = b // groups, b % groups
        column = pl.multiple_of(((x * 2 + half) * groups + g) * width, width)
        cut = pl.ds(column, width)
        both = dot(q_both, err_ref[cut, :], NT) + dot(t_both, acts_ref[:, cut], NN)
        value = both[:rank] + both[rank:]
        term[pl.ds((half * n_x * groups + b) * per, per)] = value.reshape(per, 8, width)

    for b in range(n_x * groups):
        term_block(b, mate)
    pl.semaphore_wait(barrier, len(peers))
    half_len = n_x * n_dp
    to_core = send(term.at[pl.ds(mate * half_len, half_len)], core_in, core_sem, (0,), me_dp, me_x * 2 + mate)
    to_core.start()
    for b in range(n_x * groups):
        term_block(b, core)
    to_core.wait()
    own_half = pl.ds(core * half_len, half_len)
    term[own_half] = term[own_half] + core_in[...]
    to_x = []
    for k in range(1, n_x):
        target = lax.rem(me_x + k, n_x)
        copy = send(
            term.at[pl.ds(core * half_len + target * n_dp, n_dp)], x_in.at[k], x_sem, (k,), me_dp, at_x(k)
        )
        copy.start()
        to_x.append(copy)

    loads[4].wait()
    dwidth = partial.shape[-1]

    def to_mate(b):
        return send(partial.at[b, pl.ds(mate * n_x, n_x)], partial_in.at[b], pc_sem, (b,), me_dp, me_x * 2 + mate)

    def product(b, _):
        cut = pl.ds(pl.multiple_of(b * dwidth, dwidth), dwidth)
        value = dot(cot_ref[...], weight_ref[cut, :], NT)
        step = tokens // n_t
        for tt in range(n_t):
            partial[b, (tt % 2) * n_x + tt // 2] = value[tt * step : (tt + 1) * step]
        to_mate(b).start()
        return 0

    lax.fori_loop(0, blocks, product, 0)

    own = pl.ds(core * half_len + me_x * n_dp, n_dp)
    for k, copy in enumerate(to_x, 1):
        copy.wait()
        term[own] = term[own] + x_in[k]
    to_dp = []
    for k in range(1, n_dp):
        copy = send(
            term.at[core * half_len + me_x * n_dp + at_dp(k)], dp_in.at[k], dp_sem, (k,), at_dp(k), me_t
        )
        copy.start()
        to_dp.append(copy)

    def x_copy(b, k):
        target = lax.rem(me_x + k, n_x)
        return send(partial.at[b, core * n_x + target], partial_x.at[k, b], px_sem, (k, b), me_dp, at_x(k))

    def pair_sum(b, _):
        to_mate(b).wait()
        mine = pl.ds(core * n_x, n_x)
        partial[b, mine] = partial[b, mine] + partial_in[b]
        return 0

    def x_start(b, _):
        for k in range(1, n_x):
            x_copy(b, k).start()
        return 0

    lax.fori_loop(0, early, pair_sum, 0)
    lax.fori_loop(0, early, x_start, 0)

    total = term[core * half_len + me_x * n_dp + me_dp]
    for k, copy in enumerate(to_dp, 1):
        copy.wait()
        total = total + dp_in[k]
    base = me_t * n_dp
    left_all[base + me_dp] = total
    to_all = []
    for k in range(1, n_dp):
        copy = send(left_all.at[base + me_dp], left_all.at[base + me_dp], gather_sem, (k,), at_dp(k), me_t)
        copy.start()
        to_all.append(copy)
    lax.fori_loop(early, blocks, pair_sum, 0)
    for copy in to_all:
        copy.wait()
    quarter = left_all.at[pl.ds(base, n_dp)]
    gathers = []
    for k in range(1, n_x):
        copy = send(quarter, quarter, gx_sem, (k,), me_dp, at_x(k))
        copy.start()
        gathers.append(copy)
    first = send(quarter, quarter, gcore_sem, (0,), me_dp, me_x * 2 + mate)
    first.start()
    seconds = []
    for k, copy in enumerate(gathers, 1):
        copy.wait()
        source = lax.rem(me_x - k + n_x, n_x) * 2 + core
        ref = left_all.at[pl.ds(source * n_dp, n_dp)]
        second = send(ref, ref, gcore_sem, (k,), me_dp, me_x * 2 + mate)
        second.start()
        seconds.append(second)
    lax.fori_loop(early, blocks, x_start, 0)
    first.wait()
    for copy in seconds:
        copy.wait()

    n_blocks = n_t * groups

    def left_block(b):
        return left_all[b * per : (b + 1) * per].reshape(rank, width)

    gram = jnp.zeros((rank, rank), F32)
    for b in range(n_blocks):
        block = left_block(b)
        gram += dot(block, block, NT, HI)
    inverse = inverse_factor(gram)
    u = jnp.zeros((2 * rank, tokens), F32)
    right = jnp.zeros((2 * rank, ff), F32)
    for b in range(n_blocks):
        cut = pl.ds(b * width, width)
        basis = dot(inverse, left_block(b), NN, HI)
        basis_out[:, cut] = basis
        both = jnp.concatenate(halves(basis), axis=0)
        u += dot(both, acts_ref[:, cut], NT)
        right += dot(both, err_ref[cut, :], NN)
    right += dot(jnp.concatenate(halves(u[:rank] + u[rank:]), axis=0), cot_ref[...], NN)
    right = right[:rank] + right[rank:]

    q_groups = n_dp // per
    right_part[...] = jnp.zeros_like(right_part)
    for g in range(q_groups):
        size = min(qwidth, ff - g * qwidth)
        piece = right[:, g * qwidth : g * qwidth + size]
        right_part[pl.ds(g * per, per), :, pl.ds(0, size)] = piece.reshape(per, 8, size)
    copies = []
    for k in range(1, n_dp):
        copy = send(right_part.at[at_dp(k)], right_in.at[k], r_sem, (k,), at_dp(k), me_t)
        copy.start()
        copies.append(copy)
    total = right_part[me_dp]
    for k, copy in enumerate(copies, 1):
        copy.wait()
        total = total + right_in[k]
    right_all[me_dp] = total * (1.0 / n_dp)
    copies = []
    for k in range(1, n_dp):
        copy = send(right_all.at[me_dp], right_all.at[me_dp], rg_sem, (k,), at_dp(k), me_t)
        copy.start()
        copies.append(copy)
    for copy in copies:
        copy.wait()
    for g in range(q_groups):
        size = min(qwidth, ff - g * qwidth)
        q_out[:, pl.ds(g * qwidth, size)] = right_all[pl.ds(g * per, per), :, pl.ds(0, size)].reshape(rank, size)

    def finish(b, _):
        value = partial[b, core * n_x + me_x]
        for k in range(1, n_x):
            x_copy(b, k).wait()
            value = value + partial_x[k, b]
        grad_out[:, pl.ds(pl.multiple_of(b * dwidth, dwidth), dwidth)] = value.astype(BF16)
        return 0

    lax.fori_loop(0, blocks, finish, 0)


def error_kernel(basis_ref, q_ref, acts_ref, cot_ref, err_ref, out_ref):
    bh, bl = halves(basis_ref[...])
    qh, ql = halves(q_ref[...])
    approx = dot(
        jnp.concatenate([bh, bl, bh], axis=0), jnp.concatenate([qh, qh, ql], axis=0), TN
    )
    merged = dot(acts_ref[...], cot_ref[...], TN) + err_ref[...].astype(F32)
    out_ref[...] = (merged - approx).astype(BF16)


def exchange(acts, cot, weight, err, q):
    n_dp, n_t = lax.axis_size("dp"), lax.axis_size("tensor")
    tokens, d = acts.shape
    rank, ff = q.shape
    n_x, per = n_t // 2, rank // 8
    groups = n_dp // per
    width = d // (n_t * groups)
    qwidth = ff if groups == 1 else -(-ff // (groups * 128)) * 128
    blocks, early = 8, 2
    dwidth = d // blocks
    vmem, dma = pltpu.VMEM, pltpu.SemaphoreType.DMA
    any_spec = pl.BlockSpec(memory_space=pl.ANY)
    return pl.pallas_call(
        functools.partial(exchange_kernel, (n_dp, n_t, groups, width, qwidth, blocks, early)),
        in_specs=[any_spec] * 5,
        out_specs=[pl.BlockSpec(memory_space=VMEM)] * 3,
        out_shape=(
            jax.ShapeDtypeStruct((tokens // n_t, d), BF16),
            jax.ShapeDtypeStruct((rank, d), F32),
            jax.ShapeDtypeStruct((rank, ff), F32),
        ),
        scratch_shapes=[
            vmem(q.shape, F32), vmem(cot.shape, BF16), vmem(acts.shape, BF16),
            vmem(err.shape, BF16), vmem(weight.shape, BF16),
            vmem((n_t * n_dp, 8, width), F32), vmem((n_x * n_dp, 8, width), F32),
            vmem((n_x, n_dp, 8, width), F32), vmem((n_dp, 8, width), F32),
            vmem((n_t * n_dp, 8, width), F32),
            vmem((n_dp, 8, qwidth), F32), vmem((n_dp, 8, qwidth), F32), vmem((n_dp, 8, qwidth), F32),
            vmem((blocks, n_t, tokens // n_t, dwidth), F32),
            vmem((blocks, n_x, tokens // n_t, dwidth), F32),
            vmem((n_x, blocks, tokens // n_t, dwidth), F32),
            dma((5,)), dma((2, 1)), dma((2, n_x)), dma((2, n_dp)), dma((2, n_dp)), dma((2, n_x)),
            dma((2, n_x)), dma((2, n_dp)), dma((2, n_dp)), dma((2, blocks)), dma((2, n_x, blocks)),
        ],
        compiler_params=pltpu.CompilerParams(
            collective_id=0, has_side_effects=True, vmem_limit_bytes=56 * 1024 * 1024
        ),
        name="exchange",
    )(q, cot, acts, err, weight)


def body(acts, up_cot, up_weight, error_buf, q_init):
    tokens, d = acts.shape
    rank, ff = q_init.shape
    err = error_buf[0]
    input_grad, basis, q_factor = exchange(acts, up_cot, up_weight, err, q_init)
    tile = 512
    whole = lambda shape: pl.BlockSpec(shape, lambda i: (0, 0))
    cols = lambda rows: pl.BlockSpec((rows, tile), lambda i: (0, i))
    rows = pl.BlockSpec((tile, ff), lambda i: (i, 0))
    new_error = pl.pallas_call(
        error_kernel,
        grid=(d // tile,),
        in_specs=[cols(rank), whole((rank, ff)), cols(tokens), whole((tokens, ff)), rows],
        out_specs=rows,
        out_shape=jax.ShapeDtypeStruct((d, ff), BF16),
        compiler_params=PARAMS,
        name="new_error",
    )(basis, q_factor, acts, up_cot, err)
    return (input_grad, new_error[None], basis, q_factor)


def solution(mesh):
    return jax.shard_map(
        body,
        mesh=mesh,
        in_specs=(
            P("dp", None),
            P("dp", "tensor"),
            P(None, "tensor"),
            P("dp", None, "tensor"),
            P(None, "tensor"),
        ),
        out_specs=(P(("dp", "tensor"), None), P("dp", None, "tensor"), P(), P(None, "tensor")),
        check_vma=False,
    )
```

```python
import functools

import jax
import jax.numpy as jnp
from jax import lax
from jax.experimental import pallas as pl
from jax.experimental.pallas import tpu as pltpu
from jax.sharding import PartitionSpec as P

F32 = jnp.float32
BF16 = jnp.bfloat16
VMEM = pltpu.VMEM
NT = (((1,), (1,)), ((), ()))
NN = (((1,), (0,)), ((), ()))
TN = (((0,), (0,)), ((), ()))


def dot(a, b, dims, precision=None):
    return lax.dot_general(a, b, dims, precision=precision, preferred_element_type=F32)


def halves(x):
    high = x.astype(BF16)
    low = (x - high.astype(F32)).astype(BF16)
    return high, low


def dot_split(x, b, dims):
    rows = x.shape[0]
    both = dot(jnp.concatenate(halves(x), axis=0), b, dims)
    return both[:rows] + both[rows:]


def thirds(x):
    high, rest = x.astype(BF16), x
    rest = x - high.astype(F32)
    mid, low = halves(rest)
    return high, mid, low


def inverse_factor(gram):
    n = gram.shape[0]
    row = lax.broadcasted_iota(jnp.int32, (n, n), 0)
    col = lax.broadcasted_iota(jnp.int32, (n, n), 1)
    work = jnp.concatenate([gram, (row == col).astype(F32)], axis=1)
    ids = lax.broadcasted_iota(jnp.int32, (n, 1), 0)
    scale = jnp.zeros((n, 1), F32)
    for k in range(n):
        pivot = work[k : k + 1, :]
        column = work[:, k : k + 1]
        d = work[k : k + 1, k : k + 1]
        scale = jnp.where(ids == k, d, scale)
        factor = jnp.where(ids > k, column / d, 0.0)
        work = work - factor * pivot
    return work[:, n:] * lax.rsqrt(scale)


def exchange_kernel(
    cfg,
    q_hbm, cot_hbm, acts_hbm, err_hbm, weight_hbm,
    grad_out, basis_out, q_out, error_out,
    q_ref, cot_ref, acts_ref, err_ref, weight_ref,
    term, core_in, x_in, dp_in, left_all,
    right_part, right_in, right_all,
    partial, partial_in, partial_x, merged, out_sem,
    load_sem, core_sem, x_sem, dp_sem, gather_sem, gx_sem, gcore_sem, r_sem, rg_sem, pc_sem, px_sem,
):
    n_dp, n_t, groups, width, qwidth, blocks, early = cfg
    n_x = n_t // 2
    rank, ff = q_ref.shape
    tokens = cot_ref.shape[0]
    rows_dp = rank // (n_dp // groups)
    me_dp, me_t = lax.axis_index("dp"), lax.axis_index("tensor")
    core, me_x = lax.rem(me_t, 2), lax.div(me_t, 2)
    mate = 1 - core
    per = rank // 8

    def send(src, dst, sems, index, dp, t):
        return pltpu.make_async_remote_copy(
            src_ref=src,
            dst_ref=dst,
            send_sem=sems.at[(0,) + index],
            recv_sem=sems.at[(1,) + index],
            device_id=(dp, t),
            device_id_type=pl.DeviceIdType.MESH,
        )

    def at_x(k):
        return lax.rem(me_x + k, n_x) * 2 + core

    def at_dp(k):
        return lax.rem(me_dp + k, n_dp)

    loads = [
        pltpu.make_async_copy(src, dst, load_sem.at[i])
        for i, (src, dst) in enumerate(
            ((q_hbm, q_ref), (cot_hbm, cot_ref), (acts_hbm, acts_ref), (err_hbm, err_ref), (weight_hbm, weight_ref))
        )
    ]
    for load in loads[:4]:
        load.start()

    barrier = pltpu.get_barrier_semaphore()
    peers = [(me_dp, me_x * 2 + mate)]
    peers += [(me_dp, at_x(k)) for k in range(1, n_x)]
    peers += [(at_dp(k), me_t) for k in range(1, n_dp)]
    for peer in peers:
        pl.semaphore_signal(barrier, inc=1, device_id=peer, device_id_type=pl.DeviceIdType.MESH)

    loads[0].wait()
    loads[1].wait()
    q_both = jnp.concatenate(halves(q_ref[...]), axis=0)
    t = dot(q_both, cot_ref[...], NT)
    t_both = jnp.concatenate(halves(t[:rank] + t[rank:]), axis=0)
    loads[2].wait()
    loads[3].wait()
    loads[4].start()

    def term_block(b, half):
        x, g = b // groups, b % groups
        column = pl.multiple_of(((x * 2 + half) * groups + g) * width, width)
        cut = pl.ds(column, width)
        both = dot(q_both, err_ref[cut, :], NT) + dot(t_both, acts_ref[:, cut], NN)
        value = both[:rank] + both[rank:]
        term[pl.ds((half * n_x * groups + b) * per, per)] = value.reshape(per, 8, width)

    for b in range(n_x * groups):
        term_block(b, mate)
    pl.semaphore_wait(barrier, len(peers))
    half_len = n_x * n_dp
    to_core = send(term.at[pl.ds(mate * half_len, half_len)], core_in, core_sem, (0,), me_dp, me_x * 2 + mate)
    to_core.start()
    for b in range(n_x * groups):
        term_block(b, core)
    to_core.wait()
    own_half = pl.ds(core * half_len, half_len)
    term[own_half] = term[own_half] + core_in[...]
    to_x = []
    for k in range(1, n_x):
        target = lax.rem(me_x + k, n_x)
        copy = send(
            term.at[pl.ds(core * half_len + target * n_dp, n_dp)], x_in.at[k], x_sem, (k,), me_dp, at_x(k)
        )
        copy.start()
        to_x.append(copy)

    loads[4].wait()
    dwidth = partial.shape[-1]

    def to_mate(b):
        return send(partial.at[b, pl.ds(mate * n_x, n_x)], partial_in.at[b], pc_sem, (b,), me_dp, me_x * 2 + mate)

    def product(b):
        cut = pl.ds(pl.multiple_of(b * dwidth, dwidth), dwidth)
        value = dot(cot_ref[...], weight_ref[cut, :], NT)
        step = tokens // n_t
        for tt in range(n_t):
            partial[b, (tt % 2) * n_x + tt // 2] = value[tt * step : (tt + 1) * step]
        to_mate(b).start()

    def x_copy(b, k):
        target = lax.rem(me_x + k, n_x)
        return send(
            partial.at[b, core * n_x + target], partial_x.at[k - 1, b], px_sem, (k, b), me_dp, at_x(k)
        )

    def pair_sum(b):
        to_mate(b).wait()
        mine = pl.ds(core * n_x, n_x)
        partial[b, mine] = partial[b, mine] + partial_in[b]

    def x_start(b, _):
        for k in range(1, n_x):
            x_copy(b, k).start()
        return 0

    def step(b, _):
        product(b)
        pair_sum(b - 1)
        return 0

    product(0)
    lax.fori_loop(1, blocks, step, 0)

    own = pl.ds(core * half_len + me_x * n_dp, n_dp)
    for k, copy in enumerate(to_x, 1):
        copy.wait()
        term[own] = term[own] + x_in[k]
    to_dp = []
    for k in range(1, n_dp):
        copy = send(
            term.at[core * half_len + me_x * n_dp + at_dp(k)], dp_in.at[k], dp_sem, (k,), at_dp(k), me_t
        )
        copy.start()
        to_dp.append(copy)

    lax.fori_loop(0, early, x_start, 0)
    pair_sum(blocks - 1)

    mtile = 512

    def merge(j, _):
        cut = pl.ds(pl.multiple_of(j * mtile, mtile), mtile)
        merged[cut, :] = dot(acts_ref[:, cut], cot_ref[...], TN) + err_ref[cut, :].astype(F32)
        return 0

    n_tiles = merged.shape[0] // mtile
    total = term[core * half_len + me_x * n_dp + me_dp]
    for k, copy in enumerate(to_dp, 1):
        copy.wait()
        total = total + dp_in[k]
    left_all[core, me_dp, me_x] = total
    gathers = []
    for k in range(1, n_x):
        piece = left_all.at[core, me_dp, me_x]
        copy = send(piece, piece, gx_sem, (k,), me_dp, at_x(k))
        copy.start()
        gathers.append(copy)
    for copy in gathers:
        copy.wait()
    to_all = []
    mine = left_all.at[core, me_dp]
    for k in range(1, n_dp):
        copy = send(mine, mine, gather_sem, (k,), at_dp(k), me_t)
        copy.start()
        to_all.append(copy)
    forward = [send(mine, mine, gcore_sem, (0,), me_dp, me_x * 2 + mate)]
    forward[0].start()
    lax.fori_loop(early, blocks, x_start, 0)
    lax.fori_loop(0, n_tiles // 2, merge, 0)
    for k, copy in enumerate(to_all, 1):
        copy.wait()
        ref = left_all.at[core, lax.rem(me_dp - k + n_dp, n_dp)]
        forward.append(send(ref, ref, gcore_sem, (k,), me_dp, me_x * 2 + mate))
        forward[-1].start()
    for copy in forward:
        copy.wait()

    n_blocks = n_t * groups

    def left_block(b):
        t, g = b // groups, b % groups
        return left_all[t % 2, g * per : (g + 1) * per, t // 2].reshape(rank, width)

    gram = jnp.zeros((3 * rank, 3 * rank), F32)
    for b in range(n_blocks):
        parts = jnp.concatenate(thirds(left_block(b)), axis=0)
        gram += dot(parts, parts, NT)
    gram = gram[:rank] + gram[rank : 2 * rank] + gram[2 * rank :]
    gram = gram[:, :rank] + gram[:, rank : 2 * rank] + gram[:, 2 * rank :]
    i0, i1, i2 = thirds(inverse_factor(gram))
    inverse = jnp.concatenate([i0, i0, i1, i0, i1, i2], axis=1)
    u = jnp.zeros((2 * rank, tokens), F32)
    right = jnp.zeros((2 * rank, ff), F32)
    for b in range(n_blocks):
        cut = pl.ds(b * width, width)
        l0, l1, l2 = thirds(left_block(b))
        basis = dot(inverse, jnp.concatenate([l0, l1, l0, l2, l1, l0], axis=0), NN)
        basis_out[:, cut] = basis
        both = jnp.concatenate(halves(basis), axis=0)
        u += dot(both, acts_ref[:, cut], NT)
        right += dot(both, err_ref[cut, :], NN)
    right += dot(jnp.concatenate(halves(u[:rank] + u[rank:]), axis=0), cot_ref[...], NN)
    right = right[:rank] + right[rank:]

    q_groups = n_dp // per
    right_part[...] = jnp.zeros_like(right_part)
    for g in range(q_groups):
        size = min(qwidth, ff - g * qwidth)
        piece = right[:, g * qwidth : g * qwidth + size]
        right_part[pl.ds(g * per, per), :, pl.ds(0, size)] = piece.reshape(per, 8, size)
    copies = []
    for k in range(1, n_dp):
        copy = send(right_part.at[at_dp(k)], right_in.at[k], r_sem, (k,), at_dp(k), me_t)
        copy.start()
        copies.append(copy)
    lax.fori_loop(n_tiles // 2, 3 * n_tiles // 4, merge, 0)
    total = right_part[me_dp]
    for k, copy in enumerate(copies, 1):
        copy.wait()
        total = total + right_in[k]
    right_all[me_dp] = total * (1.0 / n_dp)
    copies = []
    for k in range(1, n_dp):
        copy = send(right_all.at[me_dp], right_all.at[me_dp], rg_sem, (k,), at_dp(k), me_t)
        copy.start()
        copies.append(copy)
    lax.fori_loop(3 * n_tiles // 4, n_tiles, merge, 0)
    for copy in copies:
        copy.wait()
    for g in range(q_groups):
        size = min(qwidth, ff - g * qwidth)
        q_out[:, pl.ds(g * qwidth, size)] = right_all[pl.ds(g * per, per), :, pl.ds(0, size)].reshape(rank, size)

    qh, ql = halves(q_out[...])
    q_parts = jnp.concatenate([qh, qh, ql], axis=0)

    def store(j):
        cut = pl.ds(pl.multiple_of(j * mtile, mtile), mtile)
        return pltpu.make_async_copy(err_ref.at[cut, :], error_out.at[cut, :], out_sem.at[j])

    def subtract(j, _):
        cut = pl.ds(pl.multiple_of(j * mtile, mtile), mtile)
        bh, bl = halves(basis_out[:, cut])
        approx = dot(jnp.concatenate([bh, bl, bh], axis=0), q_parts, TN)
        err_ref[cut, :] = (merged[cut, :] - approx).astype(BF16)
        store(j).start()
        return 0

    lax.fori_loop(0, n_tiles, subtract, 0)

    def finish(b, _):
        value = partial[b, core * n_x + me_x]
        for k in range(1, n_x):
            x_copy(b, k).wait()
            value = value + partial_x[k - 1, b]
        grad_out[:, pl.ds(pl.multiple_of(b * dwidth, dwidth), dwidth)] = value.astype(BF16)
        return 0

    lax.fori_loop(0, blocks, finish, 0)

    def stored(j, _):
        store(j).wait()
        return 0

    lax.fori_loop(0, n_tiles, stored, 0)


def exchange(acts, cot, weight, err, q):
    n_dp, n_t = lax.axis_size("dp"), lax.axis_size("tensor")
    tokens, d = acts.shape
    rank, ff = q.shape
    n_x, per = n_t // 2, rank // 8
    groups = n_dp // per
    width = d // (n_t * groups)
    qwidth = ff if groups == 1 else -(-ff // (groups * 128)) * 128
    blocks, early = 8, 2
    dwidth = d // blocks
    vmem, dma = pltpu.VMEM, pltpu.SemaphoreType.DMA
    any_spec = pl.BlockSpec(memory_space=pl.ANY)
    return pl.pallas_call(
        functools.partial(exchange_kernel, (n_dp, n_t, groups, width, qwidth, blocks, early)),
        in_specs=[any_spec] * 5,
        out_specs=[pl.BlockSpec(memory_space=VMEM)] * 3 + [any_spec],
        out_shape=(
            jax.ShapeDtypeStruct((tokens // n_t, d), BF16),
            jax.ShapeDtypeStruct((rank, d), F32),
            jax.ShapeDtypeStruct((rank, ff), F32),
            jax.ShapeDtypeStruct((d, ff), BF16),
        ),
        scratch_shapes=[
            vmem(q.shape, F32), vmem(cot.shape, BF16), vmem(acts.shape, BF16),
            vmem(err.shape, BF16), vmem(weight.shape, BF16),
            vmem((n_t * n_dp, 8, width), F32), vmem((n_x * n_dp, 8, width), F32),
            vmem((n_x, n_dp, 8, width), F32), vmem((n_dp, 8, width), F32),
            vmem((2, n_dp, n_x, 8, width), F32),
            vmem((n_dp, 8, qwidth), F32), vmem((n_dp, 8, qwidth), F32), vmem((n_dp, 8, qwidth), F32),
            vmem((blocks, n_t, tokens // n_t, dwidth), F32),
            vmem((blocks, n_x, tokens // n_t, dwidth), F32),
            vmem((n_x - 1, blocks, tokens // n_t, dwidth), F32),
            vmem((d, ff), F32), dma((d // 512,)),
            dma((5,)), dma((2, 1)), dma((2, n_x)), dma((2, n_dp)), dma((2, n_dp)), dma((2, n_x)),
            dma((2, n_dp)), dma((2, n_dp)), dma((2, n_dp)), dma((2, blocks)), dma((2, n_x, blocks)),
        ],
        compiler_params=pltpu.CompilerParams(
            collective_id=0, has_side_effects=True, vmem_limit_bytes=61 * 1024 * 1024
        ),
        name="exchange",
    )(q, cot, acts, err, weight)


def body(acts, up_cot, up_weight, error_buf, q_init):
    input_grad, basis, q_factor, new_error = exchange(acts, up_cot, up_weight, error_buf[0], q_init)
    return (input_grad, new_error[None], basis, q_factor)


def solution(mesh):
    return jax.shard_map(
        body,
        mesh=mesh,
        in_specs=(
            P("dp", None),
            P("dp", "tensor"),
            P(None, "tensor"),
            P("dp", None, "tensor"),
            P(None, "tensor"),
        ),
        out_specs=(P(("dp", "tensor"), None), P("dp", None, "tensor"), P(), P(None, "tensor")),
        check_vma=False,
    )
```

```python
import functools

import jax
import jax.numpy as jnp
from jax import lax
from jax.experimental import pallas as pl
from jax.experimental.pallas import tpu as pltpu
from jax.sharding import PartitionSpec as P

F32 = jnp.float32
BF16 = jnp.bfloat16
VMEM = pltpu.VMEM
NT = (((1,), (1,)), ((), ()))
NN = (((1,), (0,)), ((), ()))
TN = (((0,), (0,)), ((), ()))


def dot(a, b, dims, precision=None):
    return lax.dot_general(a, b, dims, precision=precision, preferred_element_type=F32)


def halves(x):
    high = x.astype(BF16)
    low = (x - high.astype(F32)).astype(BF16)
    return high, low


def dot_split(x, b, dims):
    rows = x.shape[0]
    both = dot(jnp.concatenate(halves(x), axis=0), b, dims)
    return both[:rows] + both[rows:]


def thirds(x):
    high, rest = x.astype(BF16), x
    rest = x - high.astype(F32)
    mid, low = halves(rest)
    return high, mid, low


def inverse_factor(gram):
    n = gram.shape[0]
    row = lax.broadcasted_iota(jnp.int32, (n, n), 0)
    col = lax.broadcasted_iota(jnp.int32, (n, n), 1)
    work = jnp.concatenate([gram, (row == col).astype(F32)], axis=1)
    ids = lax.broadcasted_iota(jnp.int32, (n, 1), 0)
    scale = jnp.zeros((n, 1), F32)
    for k in range(n):
        pivot = work[k : k + 1, :]
        column = work[:, k : k + 1]
        d = work[k : k + 1, k : k + 1]
        scale = jnp.where(ids == k, d, scale)
        factor = jnp.where(ids > k, column / d, 0.0)
        work = work - factor * pivot
    return work[:, n:] * lax.rsqrt(scale)


def exchange_kernel(
    cfg,
    q_hbm, cot_hbm, acts_hbm, err_hbm, weight_hbm,
    grad_out, basis_out, q_out, flip_out,
    q_ref, cot_ref, acts_ref, err_ref, weight_ref,
    term, core_in, x_in, dp_in, left_all,
    right_part, right_in, right_all,
    partial, partial_in, partial_x, flipped, out_sem,
    load_sem, core_sem, x_sem, dp_sem, gather_sem, gx_sem, gcore_sem, r_sem, rg_sem, pc_sem, px_sem,
):
    n_dp, n_t, groups, width, qwidth, blocks, early = cfg
    n_x = n_t // 2
    rank, ff = q_ref.shape
    tokens = cot_ref.shape[0]
    rows_dp = rank // (n_dp // groups)
    me_dp, me_t = lax.axis_index("dp"), lax.axis_index("tensor")
    core, me_x = lax.rem(me_t, 2), lax.div(me_t, 2)
    mate = 1 - core
    per = rank // 8

    def send(src, dst, sems, index, dp, t):
        return pltpu.make_async_remote_copy(
            src_ref=src,
            dst_ref=dst,
            send_sem=sems.at[(0,) + index],
            recv_sem=sems.at[(1,) + index],
            device_id=(dp, t),
            device_id_type=pl.DeviceIdType.MESH,
        )

    def at_x(k):
        return lax.rem(me_x + k, n_x) * 2 + core

    def at_dp(k):
        return lax.rem(me_dp + k, n_dp)

    loads = [
        pltpu.make_async_copy(src, dst, load_sem.at[i])
        for i, (src, dst) in enumerate(
            ((q_hbm, q_ref), (cot_hbm, cot_ref), (acts_hbm, acts_ref), (err_hbm, err_ref), (weight_hbm, weight_ref))
        )
    ]
    for load in loads[:4]:
        load.start()

    barrier = pltpu.get_barrier_semaphore()
    peers = [(me_dp, me_x * 2 + mate)]
    peers += [(me_dp, at_x(k)) for k in range(1, n_x)]
    peers += [(at_dp(k), me_t) for k in range(1, n_dp)]
    for peer in peers:
        pl.semaphore_signal(barrier, inc=1, device_id=peer, device_id_type=pl.DeviceIdType.MESH)

    loads[0].wait()
    loads[1].wait()
    q_both = jnp.concatenate(halves(q_ref[...]), axis=0)
    t = dot(q_both, cot_ref[...], NT)
    t_both = jnp.concatenate(halves(t[:rank] + t[rank:]), axis=0)
    loads[2].wait()
    loads[3].wait()
    loads[4].start()

    def term_block(b, half):
        x, g = b // groups, b % groups
        column = pl.multiple_of(((x * 2 + half) * groups + g) * width, width)
        cut = pl.ds(column, width)
        both = dot(q_both, err_ref[cut, :], NT) + dot(t_both, acts_ref[:, cut], NN)
        value = both[:rank] + both[rank:]
        term[pl.ds((half * n_x * groups + b) * per, per)] = value.reshape(per, 8, width)

    for b in range(n_x * groups):
        term_block(b, mate)
    pl.semaphore_wait(barrier, len(peers))
    half_len = n_x * n_dp
    to_core = send(term.at[pl.ds(mate * half_len, half_len)], core_in, core_sem, (0,), me_dp, me_x * 2 + mate)
    to_core.start()
    for b in range(n_x * groups):
        term_block(b, core)
    to_core.wait()
    own_half = pl.ds(core * half_len, half_len)
    term[own_half] = term[own_half] + core_in[...]
    to_x = []
    for k in range(1, n_x):
        target = lax.rem(me_x + k, n_x)
        copy = send(
            term.at[pl.ds(core * half_len + target * n_dp, n_dp)], x_in.at[k], x_sem, (k,), me_dp, at_x(k)
        )
        copy.start()
        to_x.append(copy)

    loads[4].wait()
    dwidth = partial.shape[-1]

    def to_mate(b):
        return send(partial.at[b, pl.ds(mate * n_x, n_x)], partial_in.at[b], pc_sem, (b,), me_dp, me_x * 2 + mate)

    def product(b):
        cut = pl.ds(pl.multiple_of(b * dwidth, dwidth), dwidth)
        value = dot(cot_ref[...], weight_ref[cut, :], NT)
        step = tokens // n_t
        for tt in range(n_t):
            partial[b, (tt % 2) * n_x + tt // 2] = value[tt * step : (tt + 1) * step]
        to_mate(b).start()

    def x_copy(b, k):
        target = lax.rem(me_x + k, n_x)
        return send(
            partial.at[b, core * n_x + target], partial_x.at[k - 1, b], px_sem, (k, b), me_dp, at_x(k)
        )

    def pair_sum(b):
        to_mate(b).wait()
        mine = pl.ds(core * n_x, n_x)
        partial[b, mine] = partial[b, mine] + partial_in[b]

    def x_start(b, _):
        for k in range(1, n_x):
            x_copy(b, k).start()
        return 0

    def step(b, _):
        product(b)
        pair_sum(b - 1)
        return 0

    product(0)
    lax.fori_loop(1, blocks, step, 0)

    own = pl.ds(core * half_len + me_x * n_dp, n_dp)
    for k, copy in enumerate(to_x, 1):
        copy.wait()
        term[own] = term[own] + x_in[k]
    to_dp = []
    for k in range(1, n_dp):
        copy = send(
            term.at[core * half_len + me_x * n_dp + at_dp(k)], dp_in.at[k], dp_sem, (k,), at_dp(k), me_t
        )
        copy.start()
        to_dp.append(copy)

    lax.fori_loop(0, early, x_start, 0)
    pair_sum(blocks - 1)

    mtile = 512

    def store(j):
        cut = pl.ds(pl.multiple_of(j * mtile, mtile), mtile)
        return pltpu.make_async_copy(flipped.at[cut, :], flip_out.at[cut, :], out_sem.at[j])

    def flip(j, _):
        cut = pl.ds(pl.multiple_of(j * mtile, mtile), mtile)
        flipped[cut, :] = acts_ref[:, cut].T
        store(j).start()
        return 0

    n_tiles = flipped.shape[0] // mtile
    total = term[core * half_len + me_x * n_dp + me_dp]
    for k, copy in enumerate(to_dp, 1):
        copy.wait()
        total = total + dp_in[k]
    left_all[core, me_dp, me_x] = total
    gathers = []
    for k in range(1, n_x):
        piece = left_all.at[core, me_dp, me_x]
        copy = send(piece, piece, gx_sem, (k,), me_dp, at_x(k))
        copy.start()
        gathers.append(copy)
    for copy in gathers:
        copy.wait()
    to_all = []
    mine = left_all.at[core, me_dp]
    for k in range(1, n_dp):
        copy = send(mine, mine, gather_sem, (k,), at_dp(k), me_t)
        copy.start()
        to_all.append(copy)
    forward = [send(mine, mine, gcore_sem, (0,), me_dp, me_x * 2 + mate)]
    forward[0].start()
    lax.fori_loop(early, blocks, x_start, 0)
    lax.fori_loop(0, n_tiles, flip, 0)
    for k, copy in enumerate(to_all, 1):
        copy.wait()
        ref = left_all.at[core, lax.rem(me_dp - k + n_dp, n_dp)]
        forward.append(send(ref, ref, gcore_sem, (k,), me_dp, me_x * 2 + mate))
        forward[-1].start()
    for copy in forward:
        copy.wait()

    n_blocks = n_t * groups

    def left_block(b):
        t, g = b // groups, b % groups
        return left_all[t % 2, g * per : (g + 1) * per, t // 2].reshape(rank, width)

    gram = jnp.zeros((3 * rank, 3 * rank), F32)
    for b in range(n_blocks):
        parts = jnp.concatenate(thirds(left_block(b)), axis=0)
        gram += dot(parts, parts, NT)
    gram = gram[:rank] + gram[rank : 2 * rank] + gram[2 * rank :]
    gram = gram[:, :rank] + gram[:, rank : 2 * rank] + gram[:, 2 * rank :]
    i0, i1, i2 = thirds(inverse_factor(gram))
    inverse = jnp.concatenate([i0, i0, i1, i0, i1, i2], axis=1)
    u = jnp.zeros((2 * rank, tokens), F32)
    right = jnp.zeros((2 * rank, ff), F32)
    for b in range(n_blocks):
        cut = pl.ds(b * width, width)
        l0, l1, l2 = thirds(left_block(b))
        basis = dot(inverse, jnp.concatenate([l0, l1, l0, l2, l1, l0], axis=0), NN)
        basis_out[:, cut] = basis
        both = jnp.concatenate(halves(basis), axis=0)
        u += dot(both, acts_ref[:, cut], NT)
        right += dot(both, err_ref[cut, :], NN)
    right += dot(jnp.concatenate(halves(u[:rank] + u[rank:]), axis=0), cot_ref[...], NN)
    right = right[:rank] + right[rank:]

    q_groups = n_dp // per
    right_part[...] = jnp.zeros_like(right_part)
    for g in range(q_groups):
        size = min(qwidth, ff - g * qwidth)
        piece = right[:, g * qwidth : g * qwidth + size]
        right_part[pl.ds(g * per, per), :, pl.ds(0, size)] = piece.reshape(per, 8, size)
    copies = []
    for k in range(1, n_dp):
        copy = send(right_part.at[at_dp(k)], right_in.at[k], r_sem, (k,), at_dp(k), me_t)
        copy.start()
        copies.append(copy)
    total = right_part[me_dp]
    for k, copy in enumerate(copies, 1):
        copy.wait()
        total = total + right_in[k]
    right_all[me_dp] = total * (1.0 / n_dp)
    copies = []
    for k in range(1, n_dp):
        copy = send(right_all.at[me_dp], right_all.at[me_dp], rg_sem, (k,), at_dp(k), me_t)
        copy.start()
        copies.append(copy)
    for copy in copies:
        copy.wait()
    for g in range(q_groups):
        size = min(qwidth, ff - g * qwidth)
        q_out[:, pl.ds(g * qwidth, size)] = right_all[pl.ds(g * per, per), :, pl.ds(0, size)].reshape(rank, size)

    def finish(b, _):
        value = partial[b, core * n_x + me_x]
        for k in range(1, n_x):
            x_copy(b, k).wait()
            value = value + partial_x[k - 1, b]
        grad_out[:, pl.ds(pl.multiple_of(b * dwidth, dwidth), dwidth)] = value.astype(BF16)
        return 0

    lax.fori_loop(0, blocks, finish, 0)

    def stored(j, _):
        store(j).wait()
        return 0

    lax.fori_loop(0, n_tiles, stored, 0)


def error_kernel(
    grad_ref, basis_ref, q_ref, flip_ref, cot_ref, err_ref, grad_out, out_ref, basis_out, q_out, rhs_ref
):
    tokens = cot_ref.shape[0]

    @pl.when(pl.program_id(0) == 0)
    def _():
        qh, ql = halves(-q_ref[...])
        rhs_ref[:tokens] = cot_ref[...]
        q_out[...] = q_ref[...]
        rhs_ref[tokens:] = jnp.concatenate([qh, qh, ql, ql], axis=0)

    grad_out[...] = grad_ref[...]
    basis_out[...] = basis_ref[...]
    bh, bl = halves(basis_ref[...].T)
    lhs = jnp.concatenate([flip_ref[...], bh, bl, bh, bl], axis=1)
    out_ref[...] = (dot(lhs, rhs_ref[...], NN) + err_ref[...].astype(F32)).astype(BF16)


def exchange(acts, cot, weight, err, q):
    n_dp, n_t = lax.axis_size("dp"), lax.axis_size("tensor")
    tokens, d = acts.shape
    rank, ff = q.shape
    n_x, per = n_t // 2, rank // 8
    groups = n_dp // per
    width = d // (n_t * groups)
    qwidth = ff if groups == 1 else -(-ff // (groups * 128)) * 128
    blocks, early = 8, 2
    dwidth = d // blocks
    vmem, dma = pltpu.VMEM, pltpu.SemaphoreType.DMA
    any_spec = pl.BlockSpec(memory_space=pl.ANY)
    return pl.pallas_call(
        functools.partial(exchange_kernel, (n_dp, n_t, groups, width, qwidth, blocks, early)),
        in_specs=[any_spec] * 5,
        out_specs=[pl.BlockSpec(memory_space=VMEM)] * 3 + [any_spec],
        out_shape=(
            jax.ShapeDtypeStruct((tokens // n_t, d), BF16),
            jax.ShapeDtypeStruct((rank, d), F32),
            jax.ShapeDtypeStruct((rank, ff), F32),
            jax.ShapeDtypeStruct((d, tokens), BF16),
        ),
        scratch_shapes=[
            vmem(q.shape, F32), vmem(cot.shape, BF16), vmem(acts.shape, BF16),
            vmem(err.shape, BF16), vmem(weight.shape, BF16),
            vmem((n_t * n_dp, 8, width), F32), vmem((n_x * n_dp, 8, width), F32),
            vmem((n_x, n_dp, 8, width), F32), vmem((n_dp, 8, width), F32),
            vmem((2, n_dp, n_x, 8, width), F32),
            vmem((n_dp, 8, qwidth), F32), vmem((n_dp, 8, qwidth), F32), vmem((n_dp, 8, qwidth), F32),
            vmem((blocks, n_t, tokens // n_t, dwidth), F32),
            vmem((blocks, n_x, tokens // n_t, dwidth), F32),
            vmem((n_x - 1, blocks, tokens // n_t, dwidth), F32),
            vmem((d, tokens), BF16), dma((d // 512,)),
            dma((5,)), dma((2, 1)), dma((2, n_x)), dma((2, n_dp)), dma((2, n_dp)), dma((2, n_x)),
            dma((2, n_dp)), dma((2, n_dp)), dma((2, n_dp)), dma((2, blocks)), dma((2, n_x, blocks)),
        ],
        compiler_params=pltpu.CompilerParams(
            collective_id=0, has_side_effects=True, vmem_limit_bytes=56 * 1024 * 1024
        ),
        name="exchange",
    )(q, cot, acts, err, weight)


def body(acts, up_cot, up_weight, error_buf, q_init):
    tokens, d = acts.shape
    rank, ff = q_init.shape
    err = error_buf[0]
    input_grad, basis, q_factor, flipped = exchange(acts, up_cot, up_weight, err, q_init)
    tile = 512
    whole = lambda shape: pl.BlockSpec(shape, lambda i: (0, 0))
    rows = lambda width: pl.BlockSpec((tile, width), lambda i: (i, 0))
    cols = lambda height: pl.BlockSpec((height, tile), lambda i: (0, i))
    input_grad, new_error, basis, q_factor = pl.pallas_call(
        error_kernel,
        grid=(d // tile,),
        in_specs=[
            cols(input_grad.shape[0]), cols(rank), whole((rank, ff)),
            rows(tokens), whole((tokens, ff)), rows(ff),
        ],
        out_specs=[cols(input_grad.shape[0]), rows(ff), cols(rank), whole((rank, ff))],
        out_shape=(
            jax.ShapeDtypeStruct(input_grad.shape, BF16),
            jax.ShapeDtypeStruct((d, ff), BF16),
            jax.ShapeDtypeStruct((rank, d), F32),
            jax.ShapeDtypeStruct((rank, ff), F32),
        ),
        scratch_shapes=[pltpu.VMEM((tokens + 4 * rank, ff), BF16)],
        compiler_params=pltpu.CompilerParams(vmem_limit_bytes=56 * 1024 * 1024),
        name="new_error",
    )(input_grad, basis, q_factor, flipped, up_cot, err)
    return (input_grad, new_error[None], basis, q_factor)


def solution(mesh):
    return jax.shard_map(
        body,
        mesh=mesh,
        in_specs=(
            P("dp", None),
            P("dp", "tensor"),
            P(None, "tensor"),
            P("dp", None, "tensor"),
            P(None, "tensor"),
        ),
        out_specs=(P(("dp", "tensor"), None), P("dp", None, "tensor"), P(), P(None, "tensor")),
        check_vma=False,
    )
```

```python
import functools

import jax
import jax.numpy as jnp
from jax import lax
from jax.experimental import pallas as pl
from jax.experimental.pallas import tpu as pltpu
from jax.sharding import PartitionSpec as P

F32 = jnp.float32
BF16 = jnp.bfloat16
VMEM = pltpu.VMEM
NT = (((1,), (1,)), ((), ()))
NN = (((1,), (0,)), ((), ()))
TN = (((0,), (0,)), ((), ()))


def dot(a, b, dims, precision=None):
    return lax.dot_general(a, b, dims, precision=precision, preferred_element_type=F32)


def halves(x):
    high = x.astype(BF16)
    low = (x - high.astype(F32)).astype(BF16)
    return high, low


def dot_split(x, b, dims):
    rows = x.shape[0]
    both = dot(jnp.concatenate(halves(x), axis=0), b, dims)
    return both[:rows] + both[rows:]


def thirds(x):
    high, rest = x.astype(BF16), x
    rest = x - high.astype(F32)
    mid, low = halves(rest)
    return high, mid, low


def inverse_factor(gram):
    n = gram.shape[0]
    row = lax.broadcasted_iota(jnp.int32, (n, n), 0)
    col = lax.broadcasted_iota(jnp.int32, (n, n), 1)
    work = jnp.concatenate([gram, (row == col).astype(F32)], axis=1)
    work = [work[i : i + 8] for i in range(0, n, 8)]
    ids = lax.broadcasted_iota(jnp.int32, (8, 1), 0)
    scales = [jnp.zeros((8, 1), F32) for _ in work]
    for k in range(n):
        at, r = k // 8, k % 8
        pivot = work[at][r : r + 1, :]
        d = pivot[:, k : k + 1]
        scales[at] = jnp.where(ids == r, d, scales[at])
        scaled = pivot / d
        for g in range(at, n // 8):
            column = work[g][:, k : k + 1]
            if g == at:
                column = jnp.where(ids > r, column, 0.0)
            work[g] = work[g] - column * scaled
    return jnp.concatenate([w[:, n:] * lax.rsqrt(v) for w, v in zip(work, scales)], axis=0)


def exchange_kernel(
    cfg,
    q_hbm, cot_hbm, acts_hbm, err_hbm, weight_hbm,
    grad_out, basis_out, q_out,
    q_ref, cot_ref, acts_ref, err_ref, weight_ref,
    term, core_in, x_in, dp_in, left_all,
    right_part, right_in, right_all,
    partial, partial_in, partial_x,
    load_sem, core_sem, x_sem, dp_sem, gather_sem, gx_sem, gcore_sem, r_sem, rg_sem, pc_sem, px_sem,
):
    n_dp, n_t, groups, width, qwidth, blocks, early = cfg
    n_x = n_t // 2
    rank, ff = q_ref.shape
    tokens = cot_ref.shape[0]
    rows_dp = rank // (n_dp // groups)
    me_dp, me_t = lax.axis_index("dp"), lax.axis_index("tensor")
    core, me_x = lax.rem(me_t, 2), lax.div(me_t, 2)
    mate = 1 - core
    per = rank // 8

    def send(src, dst, sems, index, dp, t):
        return pltpu.make_async_remote_copy(
            src_ref=src,
            dst_ref=dst,
            send_sem=sems.at[(0,) + index],
            recv_sem=sems.at[(1,) + index],
            device_id=(dp, t),
            device_id_type=pl.DeviceIdType.MESH,
        )

    def at_x(k):
        return lax.rem(me_x + k, n_x) * 2 + core

    def at_dp(k):
        return lax.rem(me_dp + k, n_dp)

    n_own = n_x * groups

    def column_of(b, half):
        x, g = b // groups, b % groups
        return pl.multiple_of(((x * 2 + half) * groups + g) * width, width)

    def chunk(b, half, index):
        cut = pl.ds(column_of(b, half), width)
        return (
            pltpu.make_async_copy(err_hbm.at[cut, :], err_ref.at[cut, :], load_sem.at[3 + 2 * index]),
            pltpu.make_async_copy(acts_hbm.at[:, cut], acts_ref.at[:, cut], load_sem.at[4 + 2 * index]),
        )

    loads = [
        pltpu.make_async_copy(src, dst, load_sem.at[i])
        for i, (src, dst) in enumerate(((q_hbm, q_ref), (cot_hbm, cot_ref), (weight_hbm, weight_ref)))
    ]
    mate_chunks = [chunk(b, mate, b) for b in range(n_own)]
    own_chunks = [chunk(b, core, n_own + b) for b in range(n_own)]
    loads[0].start()
    loads[1].start()
    for pair in mate_chunks + own_chunks:
        for copy in pair:
            copy.start()

    barrier = pltpu.get_barrier_semaphore()
    peers = [(me_dp, me_x * 2 + mate)]
    peers += [(me_dp, at_x(k)) for k in range(1, n_x)]
    peers += [(at_dp(k), me_t) for k in range(1, n_dp)]
    for peer in peers:
        pl.semaphore_signal(barrier, inc=1, device_id=peer, device_id_type=pl.DeviceIdType.MESH)

    loads[0].wait()
    loads[1].wait()
    q_both = jnp.concatenate(halves(q_ref[...]), axis=0)
    t = dot(q_both, cot_ref[...], NT)
    t_both = jnp.concatenate(halves(t[:rank] + t[rank:]), axis=0)

    def term_block(b, half):
        cut = pl.ds(column_of(b, half), width)
        both = dot(q_both, err_ref[cut, :], NT) + dot(t_both, acts_ref[:, cut], NN)
        value = both[:rank] + both[rank:]
        term[pl.ds((half * n_x * groups + b) * per, per)] = value.reshape(per, 8, width)

    for b in range(n_own):
        for copy in mate_chunks[b]:
            copy.wait()
        term_block(b, mate)
    loads[2].start()
    pl.semaphore_wait(barrier, len(peers))
    half_len = n_x * n_dp
    to_core = send(term.at[pl.ds(mate * half_len, half_len)], core_in, core_sem, (0,), me_dp, me_x * 2 + mate)
    to_core.start()
    for b in range(n_own):
        for copy in own_chunks[b]:
            copy.wait()
        term_block(b, core)
    to_core.wait()
    own_half = pl.ds(core * half_len, half_len)
    term[own_half] = term[own_half] + core_in[...]
    to_x = []
    for k in range(1, n_x):
        target = lax.rem(me_x + k, n_x)
        copy = send(
            term.at[pl.ds(core * half_len + target * n_dp, n_dp)], x_in.at[k], x_sem, (k,), me_dp, at_x(k)
        )
        copy.start()
        to_x.append(copy)

    loads[2].wait()
    dwidth = partial.shape[-1]

    def to_mate(b):
        return send(partial.at[b, pl.ds(mate * n_x, n_x)], partial_in.at[b], pc_sem, (b,), me_dp, me_x * 2 + mate)

    def product(b):
        cut = pl.ds(pl.multiple_of(b * dwidth, dwidth), dwidth)
        value = dot(cot_ref[...], weight_ref[cut, :], NT)
        step = tokens // n_t
        for tt in range(n_t):
            partial[b, (tt % 2) * n_x + tt // 2] = value[tt * step : (tt + 1) * step]
        to_mate(b).start()

    def x_copy(b, k):
        target = lax.rem(me_x + k, n_x)
        return send(
            partial.at[b, core * n_x + target], partial_x.at[k - 1, b], px_sem, (k, b), me_dp, at_x(k)
        )

    def pair_sum(b):
        to_mate(b).wait()
        mine = pl.ds(core * n_x, n_x)
        partial[b, mine] = partial[b, mine] + partial_in[b]

    def x_start(b, _):
        for k in range(1, n_x):
            x_copy(b, k).start()
        return 0

    def make(b, _):
        product(b)
        return 0

    def add(b, _):
        pair_sum(b)
        return 0

    lax.fori_loop(0, blocks // 2, make, 0)
    pair_sum(0)
    x_start(0, 0)
    lax.fori_loop(blocks // 2, blocks, make, 0)

    own = pl.ds(core * half_len + me_x * n_dp, n_dp)
    for k, copy in enumerate(to_x, 1):
        copy.wait()
        term[own] = term[own] + x_in[k]
    to_dp = []
    for k in range(1, n_dp):
        copy = send(
            term.at[core * half_len + me_x * n_dp + at_dp(k)], dp_in.at[k], dp_sem, (k,), at_dp(k), me_t
        )
        copy.start()
        to_dp.append(copy)

    lax.fori_loop(1, early, add, 0)
    lax.fori_loop(1, early, x_start, 0)
    lax.fori_loop(early, blocks, add, 0)

    total = term[core * half_len + me_x * n_dp + me_dp]
    for k, copy in enumerate(to_dp, 1):
        copy.wait()
        total = total + dp_in[k]
    left_all[core, me_dp, me_x] = total
    gathers = []
    for k in range(1, n_x):
        piece = left_all.at[core, me_dp, me_x]
        copy = send(piece, piece, gx_sem, (k,), me_dp, at_x(k))
        copy.start()
        gathers.append(copy)
    for copy in gathers:
        copy.wait()
    to_all = []
    mine = left_all.at[core, me_dp]
    for k in range(1, n_dp):
        copy = send(mine, mine, gather_sem, (k,), at_dp(k), me_t)
        copy.start()
        to_all.append(copy)
    forward = [send(mine, mine, gcore_sem, (0,), me_dp, me_x * 2 + mate)]
    forward[0].start()
    lax.fori_loop(early, blocks, x_start, 0)
    for k, copy in enumerate(to_all, 1):
        copy.wait()
        ref = left_all.at[core, lax.rem(me_dp - k + n_dp, n_dp)]
        forward.append(send(ref, ref, gcore_sem, (k,), me_dp, me_x * 2 + mate))
        forward[-1].start()
    for copy in forward:
        copy.wait()

    n_blocks = n_t * groups

    def left_block(b):
        t, g = b // groups, b % groups
        return left_all[t % 2, g * per : (g + 1) * per, t // 2].reshape(rank, width)

    gram = jnp.zeros((3 * rank, 3 * rank), F32)
    for b in range(n_blocks):
        parts = jnp.concatenate(thirds(left_block(b)), axis=0)
        gram += dot(parts, parts, NT)
    gram = gram[:rank] + gram[rank : 2 * rank] + gram[2 * rank :]
    gram = gram[:, :rank] + gram[:, rank : 2 * rank] + gram[:, 2 * rank :]
    i0, i1, i2 = thirds(inverse_factor(gram))
    inverse = jnp.concatenate([i0, i0, i1, i0, i1, i2], axis=1)
    u = jnp.zeros((2 * rank, tokens), F32)
    right = jnp.zeros((2 * rank, ff), F32)
    for b in range(n_blocks):
        cut = pl.ds(b * width, width)
        l0, l1, l2 = thirds(left_block(b))
        basis = dot(inverse, jnp.concatenate([l0, l1, l0, l2, l1, l0], axis=0), NN)
        basis_out[:, cut] = basis
        both = jnp.concatenate(halves(basis), axis=0)
        u += dot(both, acts_ref[:, cut], NT)
        right += dot(both, err_ref[cut, :], NN)
    right += dot(jnp.concatenate(halves(u[:rank] + u[rank:]), axis=0), cot_ref[...], NN)
    right = right[:rank] + right[rank:]

    q_groups = n_dp // per
    right_part[...] = jnp.zeros_like(right_part)
    for g in range(q_groups):
        size = min(qwidth, ff - g * qwidth)
        piece = right[:, g * qwidth : g * qwidth + size]
        right_part[pl.ds(g * per, per), :, pl.ds(0, size)] = piece.reshape(per, 8, size)
    copies = []
    for k in range(1, n_dp):
        copy = send(right_part.at[at_dp(k)], right_in.at[k], r_sem, (k,), at_dp(k), me_t)
        copy.start()
        copies.append(copy)
    total = right_part[me_dp]
    for k, copy in enumerate(copies, 1):
        copy.wait()
        total = total + right_in[k]
    right_all[me_dp] = total * (1.0 / n_dp)
    copies = []
    for k in range(1, n_dp):
        copy = send(right_all.at[me_dp], right_all.at[me_dp], rg_sem, (k,), at_dp(k), me_t)
        copy.start()
        copies.append(copy)
    for copy in copies:
        copy.wait()
    for g in range(q_groups):
        size = min(qwidth, ff - g * qwidth)
        q_out[:, pl.ds(g * qwidth, size)] = right_all[pl.ds(g * per, per), :, pl.ds(0, size)].reshape(rank, size)

    def finish(b, _):
        value = partial[b, core * n_x + me_x]
        for k in range(1, n_x):
            x_copy(b, k).wait()
            value = value + partial_x[k - 1, b]
        grad_out[:, pl.ds(pl.multiple_of(b * dwidth, dwidth), dwidth)] = value.astype(BF16)
        return 0

    lax.fori_loop(0, blocks, finish, 0)


def error_kernel(
    grad_ref, basis_ref, q_ref, acts_ref, cot_ref, err_ref, grad_out, out_ref, basis_out, q_out, rhs_ref
):
    tokens = cot_ref.shape[0]

    @pl.when(pl.program_id(0) == 0)
    def _():
        qh, ql = halves(-q_ref[...])
        rhs_ref[:tokens] = cot_ref[...]
        q_out[...] = q_ref[...]
        rhs_ref[tokens:] = jnp.concatenate([qh, qh, ql, ql], axis=0)

    grad_out[...] = grad_ref[...]
    basis_out[...] = basis_ref[...]
    bh, bl = halves(basis_ref[...])
    lhs = jnp.concatenate([acts_ref[...], bh, bl, bh, bl], axis=0)
    out_ref[...] = (dot(lhs, rhs_ref[...], TN) + err_ref[...].astype(F32)).astype(BF16)


def exchange(acts, cot, weight, err, q):
    n_dp, n_t = lax.axis_size("dp"), lax.axis_size("tensor")
    tokens, d = acts.shape
    rank, ff = q.shape
    n_x, per = n_t // 2, rank // 8
    groups = n_dp // per
    width = d // (n_t * groups)
    qwidth = ff if groups == 1 else -(-ff // (groups * 128)) * 128
    blocks, early = 8, 2
    dwidth = d // blocks
    vmem, dma = pltpu.VMEM, pltpu.SemaphoreType.DMA
    any_spec = pl.BlockSpec(memory_space=pltpu.HBM)
    return pl.pallas_call(
        functools.partial(exchange_kernel, (n_dp, n_t, groups, width, qwidth, blocks, early)),
        in_specs=[any_spec] * 5,
        out_specs=[pl.BlockSpec(memory_space=VMEM)] * 3,
        out_shape=(
            jax.ShapeDtypeStruct((tokens // n_t, d), BF16),
            jax.ShapeDtypeStruct((rank, d), F32),
            jax.ShapeDtypeStruct((rank, ff), F32),
        ),
        scratch_shapes=[
            vmem(q.shape, F32), vmem(cot.shape, BF16), vmem(acts.shape, BF16),
            vmem(err.shape, BF16), vmem(weight.shape, BF16),
            vmem((n_t * n_dp, 8, width), F32), vmem((n_x * n_dp, 8, width), F32),
            vmem((n_x, n_dp, 8, width), F32), vmem((n_dp, 8, width), F32),
            vmem((2, n_dp, n_x, 8, width), F32),
            vmem((n_dp, 8, qwidth), F32), vmem((n_dp, 8, qwidth), F32), vmem((n_dp, 8, qwidth), F32),
            vmem((blocks, n_t, tokens // n_t, dwidth), F32),
            vmem((blocks, n_x, tokens // n_t, dwidth), F32),
            vmem((n_x - 1, blocks, tokens // n_t, dwidth), F32),
            dma((3 + 2 * n_t * groups,)), dma((2, 1)), dma((2, n_x)), dma((2, n_dp)), dma((2, n_dp)), dma((2, n_x)),
            dma((2, n_dp)), dma((2, n_dp)), dma((2, n_dp)), dma((2, blocks)), dma((2, n_x, blocks)),
        ],
        compiler_params=pltpu.CompilerParams(
            collective_id=0, has_side_effects=True, vmem_limit_bytes=43 * 1024 * 1024
        ),
        name="exchange",
    )(q, cot, acts, err, weight)


def body(acts, up_cot, up_weight, error_buf, q_init):
    tokens, d = acts.shape
    rank, ff = q_init.shape
    err = error_buf[0]
    input_grad, basis, q_factor = exchange(acts, up_cot, up_weight, err, q_init)
    tile = 512
    whole = lambda shape: pl.BlockSpec(shape, lambda i: (0, 0))
    rows = lambda width: pl.BlockSpec((tile, width), lambda i: (i, 0))
    cols = lambda height: pl.BlockSpec((height, tile), lambda i: (0, i))
    input_grad, new_error, basis, q_factor = pl.pallas_call(
        error_kernel,
        grid=(d // tile,),
        in_specs=[
            cols(input_grad.shape[0]), cols(rank), whole((rank, ff)),
            cols(tokens), whole((tokens, ff)), rows(ff),
        ],
        out_specs=[cols(input_grad.shape[0]), rows(ff), cols(rank), whole((rank, ff))],
        out_shape=(
            jax.ShapeDtypeStruct(input_grad.shape, BF16),
            jax.ShapeDtypeStruct((d, ff), BF16),
            jax.ShapeDtypeStruct((rank, d), F32),
            jax.ShapeDtypeStruct((rank, ff), F32),
        ),
        scratch_shapes=[pltpu.VMEM((tokens + 4 * rank, ff), BF16)],
        compiler_params=pltpu.CompilerParams(vmem_limit_bytes=16 * 1024 * 1024),
        name="new_error",
    )(input_grad, basis, q_factor, acts, up_cot, err)
    return (input_grad, new_error[None], basis, q_factor)


def solution(mesh):
    return jax.shard_map(
        body,
        mesh=mesh,
        in_specs=(
            P("dp", None),
            P("dp", "tensor"),
            P(None, "tensor"),
            P("dp", None, "tensor"),
            P(None, "tensor"),
        ),
        out_specs=(P(("dp", "tensor"), None), P("dp", None, "tensor"), P(), P(None, "tensor")),
        check_vma=False,
    )
```

```python
import functools

import jax
import jax.numpy as jnp
from jax import lax
from jax.experimental import pallas as pl
from jax.experimental.pallas import tpu as pltpu
from jax.sharding import PartitionSpec as P

F32 = jnp.float32
BF16 = jnp.bfloat16
VMEM = pltpu.VMEM
NT = (((1,), (1,)), ((), ()))
NN = (((1,), (0,)), ((), ()))
TN = (((0,), (0,)), ((), ()))


def dot(a, b, dims, precision=None):
    return lax.dot_general(a, b, dims, precision=precision, preferred_element_type=F32)


def halves(x):
    high = x.astype(BF16)
    low = (x - high.astype(F32)).astype(BF16)
    return high, low


def dot_split(x, b, dims):
    rows = x.shape[0]
    both = dot(jnp.concatenate(halves(x), axis=0), b, dims)
    return both[:rows] + both[rows:]


def thirds(x):
    high, rest = x.astype(BF16), x
    rest = x - high.astype(F32)
    mid, low = halves(rest)
    return high, mid, low


def inverse_factor(gram):
    n = gram.shape[0]
    row = lax.broadcasted_iota(jnp.int32, (n, n), 0)
    col = lax.broadcasted_iota(jnp.int32, (n, n), 1)
    work = jnp.concatenate([gram, (row == col).astype(F32)], axis=1)
    work = [work[i : i + 8] for i in range(0, n, 8)]
    ids = lax.broadcasted_iota(jnp.int32, (8, 1), 0)
    scales = [jnp.zeros((8, 1), F32) for _ in work]
    for k in range(n):
        at, r = k // 8, k % 8
        pivot = work[at][r : r + 1, :]
        d = pivot[:, k : k + 1]
        scales[at] = jnp.where(ids == r, d, scales[at])
        scaled = pivot / d
        for g in range(at, n // 8):
            column = work[g][:, k : k + 1]
            if g == at:
                column = jnp.where(ids > r, column, 0.0)
            work[g] = work[g] - column * scaled
    return jnp.concatenate([w[:, n:] * lax.rsqrt(v) for w, v in zip(work, scales)], axis=0)


def exchange_kernel(
    cfg,
    q_hbm, cot_hbm, acts_hbm, err_hbm, weight_hbm,
    grad_out, basis_out, q_out,
    q_ref, cot_ref, acts_ref, err_ref, weight_ref,
    term, core_in, x_in, dp_in, left_all,
    right_part, right_in, right_all,
    partial, partial_in, partial_x,
    load_sem, core_sem, x_sem, dp_sem, gather_sem, gx_sem, gcore_sem, r_sem, rg_sem, pc_sem, px_sem,
):
    n_dp, n_t, groups, width, qwidth, blocks, early = cfg
    n_x = n_t // 2
    rank, ff = q_ref.shape
    tokens = cot_ref.shape[0]
    rows_dp = rank // (n_dp // groups)
    me_dp, me_t = lax.axis_index("dp"), lax.axis_index("tensor")
    core, me_x = lax.rem(me_t, 2), lax.div(me_t, 2)
    mate = 1 - core
    per = rank // 8

    def send(src, dst, sems, index, dp, t):
        return pltpu.make_async_remote_copy(
            src_ref=src,
            dst_ref=dst,
            send_sem=sems.at[(0,) + index],
            recv_sem=sems.at[(1,) + index],
            device_id=(dp, t),
            device_id_type=pl.DeviceIdType.MESH,
        )

    def at_x(k):
        return lax.rem(me_x + k, n_x) * 2 + core

    def at_dp(k):
        return lax.rem(me_dp + k, n_dp)

    n_own = n_x * groups

    def column_of(b, half):
        x, g = b // groups, b % groups
        return pl.multiple_of(((x * 2 + half) * groups + g) * width, width)

    def chunk(b, half, index):
        cut = pl.ds(column_of(b, half), width)
        return (
            pltpu.make_async_copy(err_hbm.at[cut, :], err_ref.at[cut, :], load_sem.at[3 + 2 * index]),
            pltpu.make_async_copy(acts_hbm.at[:, cut], acts_ref.at[:, cut], load_sem.at[4 + 2 * index]),
        )

    loads = [
        pltpu.make_async_copy(src, dst, load_sem.at[i])
        for i, (src, dst) in enumerate(((q_hbm, q_ref), (cot_hbm, cot_ref), (weight_hbm, weight_ref)))
    ]
    mate_chunks = [chunk(b, mate, b) for b in range(n_own)]
    own_chunks = [chunk(b, core, n_own + b) for b in range(n_own)]
    loads[0].start()
    loads[1].start()
    for pair in mate_chunks + own_chunks:
        for copy in pair:
            copy.start()

    barrier = pltpu.get_barrier_semaphore()
    peers = [(me_dp, me_x * 2 + mate)]
    peers += [(me_dp, at_x(k)) for k in range(1, n_x)]
    peers += [(at_dp(k), me_t) for k in range(1, n_dp)]
    for peer in peers:
        pl.semaphore_signal(barrier, inc=1, device_id=peer, device_id_type=pl.DeviceIdType.MESH)

    loads[0].wait()
    loads[1].wait()
    q_both = jnp.concatenate(halves(q_ref[...]), axis=0)
    t = dot(q_both, cot_ref[...], NT)
    t_both = jnp.concatenate(halves(t[:rank] + t[rank:]), axis=0)

    def term_block(b, half):
        cut = pl.ds(column_of(b, half), width)
        both = dot(q_both, err_ref[cut, :], NT) + dot(t_both, acts_ref[:, cut], NN)
        value = both[:rank] + both[rank:]
        term[pl.ds((half * n_x * groups + b) * per, per)] = value.reshape(per, 8, width)

    for b in range(n_own):
        for copy in mate_chunks[b]:
            copy.wait()
        term_block(b, mate)
    loads[2].start()
    pl.semaphore_wait(barrier, len(peers))
    half_len = n_x * n_dp
    to_core = send(term.at[pl.ds(mate * half_len, half_len)], core_in, core_sem, (0,), me_dp, me_x * 2 + mate)
    to_core.start()
    for b in range(n_own):
        for copy in own_chunks[b]:
            copy.wait()
        term_block(b, core)
    to_core.wait()
    own_half = pl.ds(core * half_len, half_len)
    term[own_half] = term[own_half] + core_in[...]
    to_x = []
    for k in range(1, n_x):
        target = lax.rem(me_x + k, n_x)
        copy = send(
            term.at[pl.ds(core * half_len + target * n_dp, n_dp)], x_in.at[k], x_sem, (k,), me_dp, at_x(k)
        )
        copy.start()
        to_x.append(copy)

    loads[2].wait()
    dwidth = partial.shape[-1]

    def to_mate(b):
        return send(partial.at[b, pl.ds(mate * n_x, n_x)], partial_in.at[b], pc_sem, (b,), me_dp, me_x * 2 + mate)

    def product(b):
        cut = pl.ds(pl.multiple_of(b * dwidth, dwidth), dwidth)
        value = dot(cot_ref[...], weight_ref[cut, :], NT)
        step = tokens // n_t
        for tt in range(n_t):
            partial[b, (tt % 2) * n_x + tt // 2] = value[tt * step : (tt + 1) * step]
        to_mate(b).start()

    def x_copy(b, k):
        target = lax.rem(me_x + k, n_x)
        return send(
            partial.at[b, core * n_x + target], partial_x.at[k - 1, b], px_sem, (k, b), me_dp, at_x(k)
        )

    def pair_sum(b):
        to_mate(b).wait()
        mine = pl.ds(core * n_x, n_x)
        partial[b, mine] = partial[b, mine] + partial_in[b]

    def x_start(b, _):
        for k in range(1, n_x):
            x_copy(b, k).start()
        return 0

    def make(b, _):
        product(b)
        return 0

    def add(b, _):
        pair_sum(b)
        return 0

    lax.fori_loop(0, blocks // 2, make, 0)
    pair_sum(0)
    x_start(0, 0)
    lax.fori_loop(blocks // 2, blocks, make, 0)

    own = pl.ds(core * half_len + me_x * n_dp, n_dp)
    for k, copy in enumerate(to_x, 1):
        copy.wait()
        term[own] = term[own] + x_in[k]
    to_dp = []
    for k in range(1, n_dp):
        copy = send(
            term.at[core * half_len + me_x * n_dp + at_dp(k)], dp_in.at[k], dp_sem, (k,), at_dp(k), me_t
        )
        copy.start()
        to_dp.append(copy)

    lax.fori_loop(1, early, add, 0)
    lax.fori_loop(1, early, x_start, 0)
    lax.fori_loop(early, blocks, add, 0)

    total = term[core * half_len + me_x * n_dp + me_dp]
    for k, copy in enumerate(to_dp, 1):
        copy.wait()
        total = total + dp_in[k]
    left_all[core, me_dp, me_x] = total
    gathers = []
    for k in range(1, n_x):
        piece = left_all.at[core, me_dp, me_x]
        copy = send(piece, piece, gx_sem, (k,), me_dp, at_x(k))
        copy.start()
        gathers.append(copy)
    for copy in gathers:
        copy.wait()
    to_all = []
    mine = left_all.at[core, me_dp]
    for k in range(1, n_dp):
        copy = send(mine, mine, gather_sem, (k,), at_dp(k), me_t)
        copy.start()
        to_all.append(copy)
    forward = [send(mine, mine, gcore_sem, (0,), me_dp, me_x * 2 + mate)]
    forward[0].start()
    lax.fori_loop(early, blocks, x_start, 0)
    for k, copy in enumerate(to_all, 1):
        copy.wait()
        ref = left_all.at[core, lax.rem(me_dp - k + n_dp, n_dp)]
        forward.append(send(ref, ref, gcore_sem, (k,), me_dp, me_x * 2 + mate))
        forward[-1].start()
    for copy in forward:
        copy.wait()

    n_blocks = n_t * groups

    def left_block(b):
        t, g = b // groups, b % groups
        return left_all[t % 2, g * per : (g + 1) * per, t // 2].reshape(rank, width)

    def stacked(x):
        return jnp.concatenate(thirds(x), axis=0)

    def folded(x):
        return x[:rank] + x[rank : 2 * rank] + x[2 * rank :]

    def by_inverse(x):
        a0, a1, a2 = thirds(x)
        return dot(inverse, jnp.concatenate([a0, a1, a0, a2, a1, a0], axis=0), NN)

    gram = jnp.zeros((3 * rank, 3 * rank), F32)
    for b in range(n_blocks):
        parts = stacked(left_block(b))
        gram += dot(parts, parts, NT)
    gram = folded(gram)
    gram = gram[:, :rank] + gram[:, rank : 2 * rank] + gram[:, 2 * rank :]
    u = jnp.zeros((3 * rank, tokens), F32)
    right = jnp.zeros((3 * rank, ff), F32)
    for b in range(n_blocks):
        cut = pl.ds(b * width, width)
        parts = stacked(left_block(b))
        u += dot(parts, acts_ref[:, cut], NT)
        right += dot(parts, err_ref[cut, :], NN)
    right += dot(stacked(folded(u)), cot_ref[...], NN)
    i0, i1, i2 = thirds(inverse_factor(gram))
    inverse = jnp.concatenate([i0, i0, i1, i0, i1, i2], axis=1)
    right = by_inverse(folded(right))

    q_groups = n_dp // per
    right_part[...] = jnp.zeros_like(right_part)
    for g in range(q_groups):
        size = min(qwidth, ff - g * qwidth)
        piece = right[:, g * qwidth : g * qwidth + size]
        right_part[pl.ds(g * per, per), :, pl.ds(0, size)] = piece.reshape(per, 8, size)
    copies = []
    for k in range(1, n_dp):
        copy = send(right_part.at[at_dp(k)], right_in.at[k], r_sem, (k,), at_dp(k), me_t)
        copy.start()
        copies.append(copy)
    for b in range(n_blocks):
        basis_out[:, pl.ds(b * width, width)] = by_inverse(left_block(b))
    total = right_part[me_dp]
    for k, copy in enumerate(copies, 1):
        copy.wait()
        total = total + right_in[k]
    right_all[me_dp] = total * (1.0 / n_dp)
    copies = []
    for k in range(1, n_dp):
        copy = send(right_all.at[me_dp], right_all.at[me_dp], rg_sem, (k,), at_dp(k), me_t)
        copy.start()
        copies.append(copy)
    for copy in copies:
        copy.wait()
    for g in range(q_groups):
        size = min(qwidth, ff - g * qwidth)
        q_out[:, pl.ds(g * qwidth, size)] = right_all[pl.ds(g * per, per), :, pl.ds(0, size)].reshape(rank, size)

    def finish(b, _):
        value = partial[b, core * n_x + me_x]
        for k in range(1, n_x):
            x_copy(b, k).wait()
            value = value + partial_x[k - 1, b]
        grad_out[:, pl.ds(pl.multiple_of(b * dwidth, dwidth), dwidth)] = value.astype(BF16)
        return 0

    lax.fori_loop(0, blocks, finish, 0)


def error_kernel(
    grad_ref, basis_ref, q_ref, acts_ref, cot_ref, err_ref, grad_out, out_ref, basis_out, q_out, rhs_ref
):
    tokens = cot_ref.shape[0]

    @pl.when(pl.program_id(0) == 0)
    def _():
        qh, ql = halves(-q_ref[...])
        rhs_ref[:tokens] = cot_ref[...]
        q_out[...] = q_ref[...]
        rhs_ref[tokens:] = jnp.concatenate([qh, qh, ql, ql], axis=0)

    grad_out[...] = grad_ref[...]
    basis_out[...] = basis_ref[...]
    bh, bl = halves(basis_ref[...])
    lhs = jnp.concatenate([acts_ref[...], bh, bl, bh, bl], axis=0)
    out_ref[...] = (dot(lhs, rhs_ref[...], TN) + err_ref[...].astype(F32)).astype(BF16)


def exchange(acts, cot, weight, err, q):
    n_dp, n_t = lax.axis_size("dp"), lax.axis_size("tensor")
    tokens, d = acts.shape
    rank, ff = q.shape
    n_x, per = n_t // 2, rank // 8
    groups = n_dp // per
    width = d // (n_t * groups)
    qwidth = ff if groups == 1 else -(-ff // (groups * 128)) * 128
    blocks, early = 8, 3
    dwidth = d // blocks
    vmem, dma = pltpu.VMEM, pltpu.SemaphoreType.DMA
    any_spec = pl.BlockSpec(memory_space=pltpu.HBM)
    return pl.pallas_call(
        functools.partial(exchange_kernel, (n_dp, n_t, groups, width, qwidth, blocks, early)),
        in_specs=[any_spec] * 5,
        out_specs=[pl.BlockSpec(memory_space=VMEM)] * 3,
        out_shape=(
            jax.ShapeDtypeStruct((tokens // n_t, d), BF16),
            jax.ShapeDtypeStruct((rank, d), F32),
            jax.ShapeDtypeStruct((rank, ff), F32),
        ),
        scratch_shapes=[
            vmem(q.shape, F32), vmem(cot.shape, BF16), vmem(acts.shape, BF16),
            vmem(err.shape, BF16), vmem(weight.shape, BF16),
            vmem((n_t * n_dp, 8, width), F32), vmem((n_x * n_dp, 8, width), F32),
            vmem((n_x, n_dp, 8, width), F32), vmem((n_dp, 8, width), F32),
            vmem((2, n_dp, n_x, 8, width), F32),
            vmem((n_dp, 8, qwidth), F32), vmem((n_dp, 8, qwidth), F32), vmem((n_dp, 8, qwidth), F32),
            vmem((blocks, n_t, tokens // n_t, dwidth), F32),
            vmem((blocks, n_x, tokens // n_t, dwidth), F32),
            vmem((n_x - 1, blocks, tokens // n_t, dwidth), F32),
            dma((3 + 2 * n_t * groups,)), dma((2, 1)), dma((2, n_x)), dma((2, n_dp)), dma((2, n_dp)), dma((2, n_x)),
            dma((2, n_dp)), dma((2, n_dp)), dma((2, n_dp)), dma((2, blocks)), dma((2, n_x, blocks)),
        ],
        compiler_params=pltpu.CompilerParams(
            collective_id=0, has_side_effects=True, vmem_limit_bytes=43 * 1024 * 1024
        ),
        name="exchange",
    )(q, cot, acts, err, weight)


def body(acts, up_cot, up_weight, error_buf, q_init):
    tokens, d = acts.shape
    rank, ff = q_init.shape
    err = error_buf[0]
    input_grad, basis, q_factor = exchange(acts, up_cot, up_weight, err, q_init)
    tile = 512
    whole = lambda shape: pl.BlockSpec(shape, lambda i: (0, 0))
    rows = lambda width: pl.BlockSpec((tile, width), lambda i: (i, 0))
    cols = lambda height: pl.BlockSpec((height, tile), lambda i: (0, i))
    input_grad, new_error, basis, q_factor = pl.pallas_call(
        error_kernel,
        grid=(d // tile,),
        in_specs=[
            cols(input_grad.shape[0]), cols(rank), whole((rank, ff)),
            cols(tokens), whole((tokens, ff)), rows(ff),
        ],
        out_specs=[cols(input_grad.shape[0]), rows(ff), cols(rank), whole((rank, ff))],
        out_shape=(
            jax.ShapeDtypeStruct(input_grad.shape, BF16),
            jax.ShapeDtypeStruct((d, ff), BF16),
            jax.ShapeDtypeStruct((rank, d), F32),
            jax.ShapeDtypeStruct((rank, ff), F32),
        ),
        scratch_shapes=[pltpu.VMEM((tokens + 4 * rank, ff), BF16)],
        compiler_params=pltpu.CompilerParams(vmem_limit_bytes=16 * 1024 * 1024),
        name="new_error",
    )(input_grad, basis, q_factor, acts, up_cot, err)
    return (input_grad, new_error[None], basis, q_factor)


def solution(mesh):
    return jax.shard_map(
        body,
        mesh=mesh,
        in_specs=(
            P("dp", None),
            P("dp", "tensor"),
            P(None, "tensor"),
            P("dp", None, "tensor"),
            P(None, "tensor"),
        ),
        out_specs=(P(("dp", "tensor"), None), P("dp", None, "tensor"), P(), P(None, "tensor")),
        check_vma=False,
    )
```

```python
import functools

import jax
import jax.numpy as jnp
from jax import lax
from jax.experimental import pallas as pl
from jax.experimental.pallas import tpu as pltpu
from jax.sharding import PartitionSpec as P

F32 = jnp.float32
BF16 = jnp.bfloat16
VMEM = pltpu.VMEM
NT = (((1,), (1,)), ((), ()))
NN = (((1,), (0,)), ((), ()))
TN = (((0,), (0,)), ((), ()))


def dot(a, b, dims, precision=None):
    return lax.dot_general(a, b, dims, precision=precision, preferred_element_type=F32)


def halves(x):
    high = x.astype(BF16)
    low = (x - high.astype(F32)).astype(BF16)
    return high, low


def dot_split(x, b, dims):
    rows = x.shape[0]
    both = dot(jnp.concatenate(halves(x), axis=0), b, dims)
    return both[:rows] + both[rows:]


def thirds(x):
    high, rest = x.astype(BF16), x
    rest = x - high.astype(F32)
    mid, low = halves(rest)
    return high, mid, low


def inverse_factor(gram):
    n = gram.shape[0]
    row = lax.broadcasted_iota(jnp.int32, (n, n), 0)
    col = lax.broadcasted_iota(jnp.int32, (n, n), 1)
    work = jnp.concatenate([gram, (row == col).astype(F32)], axis=1)
    work = [work[i : i + 8] for i in range(0, n, 8)]
    ids = lax.broadcasted_iota(jnp.int32, (8, 1), 0)
    scales = [jnp.zeros((8, 1), F32) for _ in work]
    for k in range(n):
        at, r = k // 8, k % 8
        pivot = work[at][r : r + 1, :]
        d = pivot[:, k : k + 1]
        scales[at] = jnp.where(ids == r, d, scales[at])
        scaled = pivot / d
        for g in range(at, n // 8):
            column = work[g][:, k : k + 1]
            if g == at:
                column = jnp.where(ids > r, column, 0.0)
            work[g] = work[g] - column * scaled
    return jnp.concatenate([w[:, n:] * lax.rsqrt(v) for w, v in zip(work, scales)], axis=0)


def exchange_kernel(
    cfg,
    q_hbm, cot_hbm, acts_hbm, err_hbm, weight_hbm,
    grad_out, basis_out, q_out,
    q_ref, cot_ref, acts_ref, err_ref, weight_ref,
    term, core_in, x_in, dp_in, left_all,
    right_part, right_in, right_all,
    partial, partial_in, partial_x,
    load_sem, core_sem, x_sem, dp_sem, gather_sem, gx_sem, gcore_sem, r_sem, rg_sem, pc_sem, px_sem,
):
    n_dp, n_t, groups, width, qwidth, blocks, early = cfg
    n_x = n_t // 2
    rank, ff = q_ref.shape
    tokens = cot_ref.shape[0]
    rows_dp = rank // (n_dp // groups)
    me_dp, me_t = lax.axis_index("dp"), lax.axis_index("tensor")
    core, me_x = lax.rem(me_t, 2), lax.div(me_t, 2)
    mate = 1 - core
    per = rank // 8

    def send(src, dst, sems, index, dp, t):
        return pltpu.make_async_remote_copy(
            src_ref=src,
            dst_ref=dst,
            send_sem=sems.at[(0,) + index],
            recv_sem=sems.at[(1,) + index],
            device_id=(dp, t),
            device_id_type=pl.DeviceIdType.MESH,
        )

    def at_x(k):
        return lax.rem(me_x + k, n_x) * 2 + core

    def at_dp(k):
        return lax.rem(me_dp + k, n_dp)

    n_own = n_x * groups

    def column_of(b, half):
        x, g = b // groups, b % groups
        return pl.multiple_of(((x * 2 + half) * groups + g) * width, width)

    def chunk(b, half, index):
        cut = pl.ds(column_of(b, half), width)
        return (
            pltpu.make_async_copy(err_hbm.at[cut, :], err_ref.at[cut, :], load_sem.at[3 + 2 * index]),
            pltpu.make_async_copy(acts_hbm.at[:, cut], acts_ref.at[:, cut], load_sem.at[4 + 2 * index]),
        )

    loads = [
        pltpu.make_async_copy(src, dst, load_sem.at[i])
        for i, (src, dst) in enumerate(((q_hbm, q_ref), (cot_hbm, cot_ref), (weight_hbm, weight_ref)))
    ]
    mate_chunks = [chunk(b, mate, b) for b in range(n_own)]
    own_chunks = [chunk(b, core, n_own + b) for b in range(n_own)]
    loads[0].start()
    loads[1].start()
    for pair in mate_chunks + own_chunks:
        for copy in pair:
            copy.start()

    barrier = pltpu.get_barrier_semaphore()
    peers = [(me_dp, me_x * 2 + mate)]
    peers += [(me_dp, at_x(k)) for k in range(1, n_x)]
    peers += [(at_dp(k), me_t) for k in range(1, n_dp)]
    for peer in peers:
        pl.semaphore_signal(barrier, inc=1, device_id=peer, device_id_type=pl.DeviceIdType.MESH)

    loads[0].wait()
    loads[1].wait()
    q_both = jnp.concatenate(halves(q_ref[...]), axis=0)
    t = dot(q_both, cot_ref[...], NT)
    t_both = jnp.concatenate(halves(t[:rank] + t[rank:]), axis=0)

    def term_block(b, half):
        cut = pl.ds(column_of(b, half), width)
        both = dot(q_both, err_ref[cut, :], NT) + dot(t_both, acts_ref[:, cut], NN)
        value = both[:rank] + both[rank:]
        term[pl.ds((half * n_x * groups + b) * per, per)] = value.reshape(per, 8, width)

    for b in range(n_own):
        for copy in mate_chunks[b]:
            copy.wait()
        term_block(b, mate)
    loads[2].start()
    pl.semaphore_wait(barrier, len(peers))
    half_len = n_x * n_dp
    to_core = send(term.at[pl.ds(mate * half_len, half_len)], core_in, core_sem, (0,), me_dp, me_x * 2 + mate)
    to_core.start()
    for b in range(n_own):
        for copy in own_chunks[b]:
            copy.wait()
        term_block(b, core)
    to_core.wait()
    own_half = pl.ds(core * half_len, half_len)
    term[own_half] = term[own_half] + core_in[...]
    to_x = []
    for k in range(1, n_x):
        target = lax.rem(me_x + k, n_x)
        copy = send(
            term.at[pl.ds(core * half_len + target * n_dp, n_dp)], x_in.at[k], x_sem, (k,), me_dp, at_x(k)
        )
        copy.start()
        to_x.append(copy)

    loads[2].wait()
    dwidth = partial.shape[-1]

    def to_mate(b):
        return send(partial.at[b, pl.ds(mate * n_x, n_x)], partial_in.at[b], pc_sem, (b,), me_dp, me_x * 2 + mate)

    def product(b):
        cut = pl.ds(pl.multiple_of(b * dwidth, dwidth), dwidth)
        value = dot(cot_ref[...], weight_ref[cut, :], NT)
        step = tokens // n_t
        for tt in range(n_t):
            partial[b, (tt % 2) * n_x + tt // 2] = value[tt * step : (tt + 1) * step]
        to_mate(b).start()

    def x_copy(b, k):
        target = lax.rem(me_x + k, n_x)
        return send(
            partial.at[b, core * n_x + target], partial_x.at[k - 1, b], px_sem, (k, b), me_dp, at_x(k)
        )

    def pair_sum(b):
        to_mate(b).wait()
        mine = pl.ds(core * n_x, n_x)
        partial[b, mine] = partial[b, mine] + partial_in[b]

    def x_start(b, _):
        for k in range(1, n_x):
            x_copy(b, k).start()
        return 0

    def make(b, _):
        product(b)
        return 0

    def add(b, _):
        pair_sum(b)
        return 0

    lax.fori_loop(0, blocks // 2, make, 0)
    pair_sum(0)
    x_start(0, 0)
    lax.fori_loop(blocks // 2, blocks, make, 0)

    own = pl.ds(core * half_len + me_x * n_dp, n_dp)
    for k, copy in enumerate(to_x, 1):
        copy.wait()
        term[own] = term[own] + x_in[k]
    to_dp = []
    for k in range(1, n_dp):
        copy = send(
            term.at[core * half_len + me_x * n_dp + at_dp(k)], dp_in.at[k], dp_sem, (k,), at_dp(k), me_t
        )
        copy.start()
        to_dp.append(copy)

    lax.fori_loop(1, early, add, 0)
    lax.fori_loop(1, early, x_start, 0)
    lax.fori_loop(early, blocks, add, 0)

    total = term[core * half_len + me_x * n_dp + me_dp]
    for k, copy in enumerate(to_dp, 1):
        copy.wait()
        total = total + dp_in[k]
    left_all[core, me_dp, me_x] = total
    gathers = []
    for k in range(1, n_x):
        piece = left_all.at[core, me_dp, me_x]
        copy = send(piece, piece, gx_sem, (k,), me_dp, at_x(k))
        copy.start()
        gathers.append(copy)
    for copy in gathers:
        copy.wait()
    to_all = []
    mine = left_all.at[core, me_dp]
    for k in range(1, n_dp):
        copy = send(mine, mine, gather_sem, (k,), at_dp(k), me_t)
        copy.start()
        to_all.append(copy)
    forward = [send(mine, mine, gcore_sem, (0,), me_dp, me_x * 2 + mate)]
    forward[0].start()
    lax.fori_loop(early, blocks, x_start, 0)
    for k, copy in enumerate(to_all, 1):
        copy.wait()
        ref = left_all.at[core, lax.rem(me_dp - k + n_dp, n_dp)]
        forward.append(send(ref, ref, gcore_sem, (k,), me_dp, me_x * 2 + mate))
        forward[-1].start()
    for copy in forward:
        copy.wait()

    n_blocks = n_t * groups

    def left_block(b):
        t, g = b // groups, b % groups
        return left_all[t % 2, g * per : (g + 1) * per, t // 2].reshape(rank, width)

    def stacked(x):
        return jnp.concatenate(thirds(x), axis=0)

    def folded(x):
        return x[:rank] + x[rank : 2 * rank] + x[2 * rank :]

    def by_inverse(x):
        a0, a1, a2 = thirds(x)
        return dot(inverse, jnp.concatenate([a0, a1, a0, a2, a1, a0], axis=0), NN)

    gram = jnp.zeros((3 * rank, 3 * rank), F32)
    for b in range(n_blocks):
        parts = stacked(left_block(b))
        gram += dot(parts, parts, NT)
    gram = folded(gram)
    gram = gram[:, :rank] + gram[:, rank : 2 * rank] + gram[:, 2 * rank :]
    u = jnp.zeros((3 * rank, tokens), F32)
    right = jnp.zeros((3 * rank, ff), F32)
    for b in range(n_blocks):
        cut = pl.ds(b * width, width)
        parts = stacked(left_block(b))
        u += dot(parts, acts_ref[:, cut], NT)
        right += dot(parts, err_ref[cut, :], NN)
    right += dot(stacked(folded(u)), cot_ref[...], NN)
    i0, i1, i2 = thirds(inverse_factor(gram))
    inverse = jnp.concatenate([i0, i0, i1, i0, i1, i2], axis=1)
    right = by_inverse(folded(right))

    q_groups = n_dp // per
    right_part[...] = jnp.zeros_like(right_part)
    for g in range(q_groups):
        size = min(qwidth, ff - g * qwidth)
        piece = right[:, g * qwidth : g * qwidth + size]
        right_part[pl.ds(g * per, per), :, pl.ds(0, size)] = piece.reshape(per, 8, size)
    copies = []
    for k in range(1, n_dp):
        copy = send(right_part.at[at_dp(k)], right_in.at[k], r_sem, (k,), at_dp(k), me_t)
        copy.start()
        copies.append(copy)
    for b in range(n_blocks):
        basis_out[:, pl.ds(b * width, width)] = by_inverse(left_block(b))
    total = right_part[me_dp]
    for k, copy in enumerate(copies, 1):
        copy.wait()
        total = total + right_in[k]
    right_all[me_dp] = total * (1.0 / n_dp)
    copies = []
    for k in range(1, n_dp):
        copy = send(right_all.at[me_dp], right_all.at[me_dp], rg_sem, (k,), at_dp(k), me_t)
        copy.start()
        copies.append(copy)
    for copy in copies:
        copy.wait()
    for g in range(q_groups):
        size = min(qwidth, ff - g * qwidth)
        q_out[:, pl.ds(g * qwidth, size)] = right_all[pl.ds(g * per, per), :, pl.ds(0, size)].reshape(rank, size)

    def finish(b, _):
        value = partial[b, core * n_x + me_x]
        for k in range(1, n_x):
            x_copy(b, k).wait()
            value = value + partial_x[k - 1, b]
        grad_out[:, pl.ds(pl.multiple_of(b * dwidth, dwidth), dwidth)] = value.astype(BF16)
        return 0

    lax.fori_loop(0, blocks, finish, 0)


def error_kernel(
    grad_ref, basis_ref, q_ref, acts_ref, cot_ref, err_ref, grad_out, out_ref, basis_out, q_out, rhs_ref
):
    tokens = cot_ref.shape[0]

    @pl.when(pl.program_id(0) == 0)
    def _():
        qh, ql = halves(-q_ref[...])
        rhs_ref[:tokens] = cot_ref[...]
        q_out[...] = q_ref[...]
        rhs_ref[tokens:] = jnp.concatenate([qh, qh, ql, ql], axis=0)

    grad_out[...] = grad_ref[...]
    basis_out[...] = basis_ref[...]
    bh, bl = halves(basis_ref[...])
    lhs = jnp.concatenate([acts_ref[...], bh, bl, bh, bl], axis=0)
    out_ref[...] = (dot(lhs, rhs_ref[...], TN) + err_ref[...].astype(F32)).astype(BF16)


def exchange(acts, cot, weight, err, q):
    n_dp, n_t = lax.axis_size("dp"), lax.axis_size("tensor")
    tokens, d = acts.shape
    rank, ff = q.shape
    n_x, per = n_t // 2, rank // 8
    groups = n_dp // per
    width = d // (n_t * groups)
    qwidth = ff if groups == 1 else -(-ff // (groups * 128)) * 128
    blocks, early = 8, 1
    dwidth = d // blocks
    vmem, dma = pltpu.VMEM, pltpu.SemaphoreType.DMA
    any_spec = pl.BlockSpec(memory_space=pltpu.HBM)
    return pl.pallas_call(
        functools.partial(exchange_kernel, (n_dp, n_t, groups, width, qwidth, blocks, early)),
        in_specs=[any_spec] * 5,
        out_specs=[pl.BlockSpec(memory_space=VMEM)] * 3,
        out_shape=(
            jax.ShapeDtypeStruct((tokens // n_t, d), BF16),
            jax.ShapeDtypeStruct((rank, d), F32),
            jax.ShapeDtypeStruct((rank, ff), F32),
        ),
        scratch_shapes=[
            vmem(q.shape, F32), vmem(cot.shape, BF16), vmem(acts.shape, BF16),
            vmem(err.shape, BF16), vmem(weight.shape, BF16),
            vmem((n_t * n_dp, 8, width), F32), vmem((n_x * n_dp, 8, width), F32),
            vmem((n_x, n_dp, 8, width), F32), vmem((n_dp, 8, width), F32),
            vmem((2, n_dp, n_x, 8, width), F32),
            vmem((n_dp, 8, qwidth), F32), vmem((n_dp, 8, qwidth), F32), vmem((n_dp, 8, qwidth), F32),
            vmem((blocks, n_t, tokens // n_t, dwidth), F32),
            vmem((blocks, n_x, tokens // n_t, dwidth), F32),
            vmem((n_x - 1, blocks, tokens // n_t, dwidth), F32),
            dma((3 + 2 * n_t * groups,)), dma((2, 1)), dma((2, n_x)), dma((2, n_dp)), dma((2, n_dp)), dma((2, n_x)),
            dma((2, n_dp)), dma((2, n_dp)), dma((2, n_dp)), dma((2, blocks)), dma((2, n_x, blocks)),
        ],
        compiler_params=pltpu.CompilerParams(
            collective_id=0, has_side_effects=True, vmem_limit_bytes=43 * 1024 * 1024
        ),
        name="exchange",
    )(q, cot, acts, err, weight)


def body(acts, up_cot, up_weight, error_buf, q_init):
    tokens, d = acts.shape
    rank, ff = q_init.shape
    err = error_buf[0]
    input_grad, basis, q_factor = exchange(acts, up_cot, up_weight, err, q_init)
    tile = 512
    whole = lambda shape: pl.BlockSpec(shape, lambda i: (0, 0))
    rows = lambda width: pl.BlockSpec((tile, width), lambda i: (i, 0))
    cols = lambda height: pl.BlockSpec((height, tile), lambda i: (0, i))
    input_grad, new_error, basis, q_factor = pl.pallas_call(
        error_kernel,
        grid=(d // tile,),
        in_specs=[
            cols(input_grad.shape[0]), cols(rank), whole((rank, ff)),
            cols(tokens), whole((tokens, ff)), rows(ff),
        ],
        out_specs=[cols(input_grad.shape[0]), rows(ff), cols(rank), whole((rank, ff))],
        out_shape=(
            jax.ShapeDtypeStruct(input_grad.shape, BF16),
            jax.ShapeDtypeStruct((d, ff), BF16),
            jax.ShapeDtypeStruct((rank, d), F32),
            jax.ShapeDtypeStruct((rank, ff), F32),
        ),
        scratch_shapes=[pltpu.VMEM((tokens + 4 * rank, ff), BF16)],
        compiler_params=pltpu.CompilerParams(vmem_limit_bytes=16 * 1024 * 1024),
        name="new_error",
    )(input_grad, basis, q_factor, acts, up_cot, err)
    return (input_grad, new_error[None], basis, q_factor)


def solution(mesh):
    return jax.shard_map(
        body,
        mesh=mesh,
        in_specs=(
            P("dp", None),
            P("dp", "tensor"),
            P(None, "tensor"),
            P("dp", None, "tensor"),
            P(None, "tensor"),
        ),
        out_specs=(P(("dp", "tensor"), None), P("dp", None, "tensor"), P(), P(None, "tensor")),
        check_vma=False,
    )
```
